512 devices in a mesh: dp: 32 (over z, core), expert: 16 (over y, x).
Axes of the slice: x: 4, y: 4, z: 16, core: 2. Of those that a mesh axis runs over, the one named last changes fastest.
Arguments:
- attn_input: bfloat16 [65536, 3072], P(('dp', 'expert')), may hold values from -24 to 24
- key_cot: bfloat16 [65536, 512], P(('dp', 'expert')), may hold values from -6 to 6
- routing: int32 [65536, 4], P(('dp', 'expert')), may hold values from 0 to 15, all different within a row; in each aligned block of 128 rows (0 to 127, 128 to 255, ...) at most 34 rows name the same one
- router_base: float32 [65536, 16], P(('dp', 'expert')), may hold values from -1.5 to 1.5
- router_weight: bfloat16 [3072, 16], replicated, may hold values from -1.5 to 1.5
- expert_rows: bfloat16 [8192, 34, 3072], P(('dp', 'expert')), may hold values from -6 to 6
- expert_dots: bfloat16 [8192, 34], P(('dp', 'expert')), may hold values from -16 to 16
- key_weight: float32 [3072, 512], P(('dp', 'expert')), may hold values from -0.25 to 0.25
- first_moment: float32 [3072, 512], P(('dp', 'expert')), may hold values from -1536 to 1536
- second_moment: float32 [3072, 512], P(('dp', 'expert')), may hold values from 13107.2 to 327680
Outputs:
- input_grad: bfloat16 [65536, 3072], P(('dp', 'expert'))
- new_key_weight: float32 [3072, 512], P(('dp', 'expert'))
- new_first_moment: float32 [3072, 512], P(('dp', 'expert'))
- new_second_moment: float32 [3072, 512], P(('dp', 'expert'))
The draws below stay inside these ranges and needn't reach their ends.
Inputs may be any that keep to these rules, and one draw needn't show every extreme that they name: `routing`: each token names 4 different experts. The 128 tokens of one device name any one expert at most 34 times, and that bound is reached.
All inputs are finite; a program needn't handle non-finite values.
Results may differ from the reference program's by a relative error of at most 0.0043.
Values may be sent and summed in bfloat16 or wider, within the bound.
No kernel may reach another device: no remote copies, remote signals or barrier semaphores. Data moves between devices by JAX's collectives and lax.ppermute only.
A program may use at most 64 MiB of HBM per device.

```python
import math
import jax
import jax.numpy as jnp
import numpy as np
from jax import lax

D = 3072
TOP = 4
ADAM_STEP = 10
TOK_DEV = 128
EXPERTS = 16
KCOLS = 512
CAP = 34
TOKENS = 65536
N_DP = 32
N_EXPERT = 16


def strengthened(entries, rng, source, target, parts, factor):
    def block_of(dim):
        return (jnp.arange(entries.shape[dim]) // (entries.shape[dim] // parts)).reshape((-1,) + (1,) * (entries.ndim - 1 - dim))

    first = jax.random.permutation(rng, parts)[block_of(target)]
    far = (block_of(target) + parts // 2) % parts
    return jnp.where((block_of(source) == first) | (block_of(source) == far), factor * entries, entries)


def levels(key, extent, split, smallest, top_value):
    level, own = 1.0, jax.random.fold_in(key, 6)
    for dim, shards_of in split:
        draws = jnp.exp(jax.random.uniform(jax.random.fold_in(own, dim), (shards_of,), jnp.float32, smallest / len(split), top_value / len(split)))
        level = level * jnp.repeat(draws, extent[dim] // shards_of).reshape([-1 if axis == dim else 1 for axis in range(len(extent))])
    return level


def shared_out(stream_key, own, number, rows, number_of, top, bound, lean):
    sequence = jax.random.permutation(stream_key, number_of)
    crowded, ordinary = portions_of(number_of, rows * top, bound, lean, True), portions_of(number_of, rows * top, bound, lean, False)
    places = jnp.arange(number_of)

    def named(tallies, turn):
        used = int((tallies > 0).sum())
        fixed = max(1, used // 4)
        shifted = fixed + (places - fixed + turn * (used - fixed)) % max(1, number_of - fixed)
        return jnp.zeros((number_of,), jnp.int32).at[sequence[jnp.where(places < fixed, places, shifted)]].set(jnp.asarray(tallies, jnp.int32))

    tallies = jnp.where(number % 4 == 0, named(crowded, number // 4), named(ordinary, number - number // 4 - 1))
    mixed = jax.random.permutation(jax.random.fold_in(own, 3), number_of)
    donor, taker = mixed[0:number_of // 2 * 2:2], mixed[1:number_of // 2 * 2:2]
    room = jnp.minimum(tallies[donor] - 1, bound - tallies[taker]) // 2
    room = jnp.where((donor == sequence[0]) | (taker == sequence[0]) | (tallies[taker] == 0), 0, jnp.maximum(room, 0))
    shifted = jax.random.randint(jax.random.fold_in(own, 4), (number_of // 2,), 0, 1 << 20) % (room + 1)
    tallies = tallies.at[donor].add(-shifted).at[taker].add(shifted)
    items = jnp.searchsorted(jnp.cumsum(tallies), jnp.arange(rows * top), side="right").astype(jnp.int32)
    grid = items.reshape(top, rows).T
    grid = grid[jax.random.permutation(jax.random.fold_in(own, 1), rows)]
    turn = jax.random.randint(jax.random.fold_in(own, 2), (rows, 1), 0, top)
    return jnp.take_along_axis(grid, (jnp.arange(top)[None, :] + turn) % top, axis=1)


def portions_of(amount, total, limit, slope, full):
    portions = [(1 << 20) // math.isqrt(standing ** slope) + 1 for standing in range(1, amount + 1)]
    largest = limit if full else min(limit, max(-(-total // amount), total * portions[0] // sum(portions)))
    least = 1 if total - largest >= amount - 1 else 0
    holding, rest = [largest] + [least] * (amount - 1), total - largest - least * (amount - 1)
    while rest > 0:
        free = [i for i in range(1, amount) if holding[i] < largest] or [i for i in range(1, amount) if holding[i] < limit]
        mass, left = sum([portions[i] for i in free]), rest
        for i in free:
            more = min(limit - holding[i], max(1, left * portions[i] // mass), rest)
            holding[i] = holding[i] + more
            rest = rest - more
    return np.array(holding)


def centred(key, dims, spread, limit, cuts=(), kind=jnp.bfloat16):
    values = jax.random.normal(key, dims, jnp.float32) * spread
    if len(cuts) > 0:
        values = levels(key, dims, cuts, -0.22, 0.18) * values
    return jnp.clip(values, min=-limit, max=limit).astype(kind)


def gaussian_with(key, shape, scale, limit, split, heavy, kind=jnp.bfloat16):
    drawn = scale * jax.random.normal(key, shape, jnp.float32)
    if split:
        drawn = drawn * levels(key, shape, split, -0.22, 0.18)
    return jnp.clip(strengthened(drawn, jax.random.fold_in(key, 3), *heavy), -limit, limit).astype(kind)


def setup_inputs(seed: int = 0) -> dict:
    seeds = jax.random.split(jax.random.key(seed), 11)
    attn_input = gaussian_with(seeds[0], (TOKENS, D), 1.0, 24.0, ((0, 512),), (0, 1, 512, 6.0))
    key_cot = centred(seeds[1], (TOKENS, KCOLS), 1.0, 6.0, ((0, 512),))
    routing_keys = jax.random.split(jax.random.fold_in(seeds[2], 1), TOKENS // TOK_DEV)
    routing_turns = jax.random.permutation(jax.random.fold_in(seeds[2], 3), TOKENS // TOK_DEV)
    routing = jax.vmap(lambda own, number: shared_out(jax.random.fold_in(seeds[2], 2), own, number, TOK_DEV, EXPERTS, TOP, CAP, 1))(routing_keys, routing_turns).reshape((TOKENS, TOP))
    router_base = jnp.clip(jax.random.uniform(seeds[3], (TOKENS, EXPERTS), jnp.float32, -1.5, 1.5) * levels(seeds[3], (TOKENS, EXPERTS), ((0, 512),), -0.4, 0.0), -1.5, 1.5)
    router_weight = centred(seeds[4], (D, EXPERTS), EXPERTS ** -0.5, 1.5)
    expert_rows = centred(seeds[5], (N_DP * EXPERTS * EXPERTS, CAP, D), 1.0, 6.0, ((0, 512),))
    expert_dots = centred(seeds[6], (N_DP * EXPERTS * EXPERTS, CAP), 4.0, 16.0, ((0, 512),))
    key_weight = centred(seeds[7], (D, KCOLS), KCOLS ** -0.5, 0.25, ((0, 512),), jnp.float32)
    first_moment = centred(seeds[8], (D, KCOLS), (TOKENS ** 0.5), 1536.0, ((0, 512),), jnp.float32)
    second_moment = jnp.clip(jnp.exp(math.log(327680.0) - 3.218876 * jax.random.uniform(seeds[9], (D, KCOLS), jnp.float32) ** levels(seeds[9], (D, KCOLS), ((0, 512),), -0.2, 0.2)), 13107.2, 327680.0)
    return {"attn_input": attn_input, "key_cot": key_cot, "routing": routing, "router_base": router_base, "router_weight": router_weight, "expert_rows": expert_rows, "expert_dots": expert_dots, "key_weight": key_weight, "first_moment": first_moment, "second_moment": second_moment}


beta_one = 0.9
beta_two = 0.95
epsilon = 1e-08
learn_rate = 0.005
decay_rate = 0.1
routed_offset = 3.5

def route_slots(routing, experts, capacity):
    choose = (routing[:, :, None] == jnp.arange(experts, dtype=jnp.int32)[None, None, :]).astype(jnp.int32)
    per_expert = lax.optimization_barrier(jnp.sum(choose, axis=1))
    before = jnp.cumsum(per_expert, axis=0) - per_expert
    slots = lax.optimization_barrier(jnp.sum(choose * before[:, None, :], axis=2))
    return (choose, routing * capacity + slots)

def combine(routing, router_base, returned, returned_dots, router_weight):
    experts, capacity, features = returned.shape
    choose, flat_index = route_slots(routing, experts, capacity)
    routed_mask = lax.optimization_barrier(jnp.sum(choose, axis=1)).astype(jnp.float32)
    router_probs = jax.nn.softmax(router_base + routed_offset * routed_mask, axis=-1)
    picked = jnp.take(returned.reshape(experts * capacity, features), flat_index, axis=0)
    inner = jnp.take(returned_dots.reshape(experts * capacity), flat_index, axis=0).astype(jnp.float32)
    chosen = jnp.take_along_axis(router_probs, routing, axis=1)
    chosen_sum = lax.optimization_barrier(jnp.sum(chosen, axis=1, keepdims=True))
    gate_share = chosen / chosen_sum
    mixed = gate_share[:, 0:1] * picked[:, 0].astype(jnp.float32)
    for position in range(1, routing.shape[1]):
        mixed = mixed + gate_share[:, position:position + 1] * picked[:, position].astype(jnp.float32)
    mean_inner = lax.optimization_barrier(jnp.sum(gate_share * inner, axis=1, keepdims=True))
    d_chosen = (inner - mean_inner) / chosen_sum
    d_probs = lax.optimization_barrier(jnp.sum(choose.astype(jnp.float32) * d_chosen[:, :, None], axis=1))
    d_logits = router_probs * (d_probs - lax.optimization_barrier(jnp.sum(router_probs * d_probs, axis=1, keepdims=True)))
    router_term = jnp.dot(d_logits, router_weight.astype(jnp.float32).T, precision=lax.Precision.HIGHEST)
    return mixed + router_term

def adamw(weight, first, second, grad):
    new_first = beta_one * first + (1.0 - beta_one) * grad
    new_second = beta_two * second + (1.0 - beta_two) * grad * grad
    first_hat = new_first / (1.0 - beta_one ** ADAM_STEP)
    second_hat = new_second / (1.0 - beta_two ** ADAM_STEP)
    new_weight = weight - learn_rate * (first_hat / (jnp.sqrt(second_hat) + epsilon) + decay_rate * weight)
    return (new_weight, new_first, new_second)

def reference(attn_input, key_cot, routing, router_base, router_weight, expert_rows, expert_dots, key_weight, first_moment, second_moment):
    devices = N_DP * N_EXPERT
    rows_all = expert_rows.reshape(N_DP, EXPERTS, EXPERTS, CAP, D)
    dots_all = expert_dots.reshape(N_DP, EXPERTS, EXPERTS, CAP)
    inputs = attn_input.reshape(devices, TOK_DEV, D)
    cotangents = key_cot.reshape(devices, TOK_DEV, KCOLS)
    routes = routing.reshape(devices, TOK_DEV, TOP)
    base_all = router_base.reshape(devices, TOK_DEV, EXPERTS)
    key_wide = key_weight.astype(jnp.bfloat16).astype(jnp.float32)

    def one_device(running, index):
        cycle_index = index // N_EXPERT
        source = index % N_EXPERT
        returned = lax.dynamic_index_in_dim(rows_all, cycle_index, 0, False)
        returned = lax.dynamic_index_in_dim(returned, source, 1, False)
        returned_dots = lax.dynamic_index_in_dim(dots_all, cycle_index, 0, False)
        returned_dots = lax.dynamic_index_in_dim(returned_dots, source, 1, False)
        own_routes = lax.dynamic_index_in_dim(routes, index, 0, False)
        own_base = lax.dynamic_index_in_dim(base_all, index, 0, False)
        cotangent = lax.dynamic_index_in_dim(cotangents, index, 0, False).astype(jnp.float32)
        own_input = lax.dynamic_index_in_dim(inputs, index, 0, False).astype(jnp.float32)
        moe_term = combine(own_routes, own_base, returned, returned_dots, router_weight)
        key_term = jnp.dot(cotangent, key_wide.T, precision=lax.Precision.HIGHEST)
        grad_rows = (moe_term + key_term).astype(jnp.bfloat16)
        partial_grad = jnp.dot(own_input.T, cotangent, precision=lax.Precision.HIGHEST)
        partial_grad = lax.optimization_barrier(partial_grad.astype(jnp.bfloat16)).astype(jnp.float32)
        return (running + partial_grad, grad_rows)
    key_grad, grads = lax.scan(one_device, jnp.zeros((D, KCOLS), jnp.float32), jnp.arange(devices, dtype=jnp.int32))
    input_grad = grads.reshape(TOKENS, D)
    new_key_weight, new_first_moment, new_second_moment = adamw(key_weight, first_moment, second_moment, key_grad)
    return (input_grad, new_key_weight, new_first_moment, new_second_moment)
```

```python
import jax
import jax.numpy as jnp
from jax import lax
from jax.experimental import pallas as pl
from jax.experimental.pallas import tpu as pltpu
from jax.sharding import PartitionSpec as P

ADAM_STEP = 10

beta_one = 0.9
beta_two = 0.95
epsilon = 1e-08
learn_rate = 0.005
decay_rate = 0.1
routed_offset = 3.5

BF = jnp.bfloat16
F32 = jnp.float32

TOK, D, KC = 128, 3072, 512
EXP, CAP = 16, 34
HEAD = 32
REST = CAP - HEAD
PARTS = 8
COLS = D // PARTS
CHUNK = PARTS * CAP
ZN, CORES, SUB = 16, 2, 6
DPROWS = EXP * SUB

VM = pltpu.VMEM
HB = pl.ANY


def iota(shape, dim):
    return lax.broadcasted_iota(jnp.int32, shape, dim)


def dot(a, b, ca=1, cb=0):
    return lax.dot_general(a, b, (((ca,), (cb,)), ((), ())), preferred_element_type=F32)


def params(mib):
    return pltpu.CompilerParams(vmem_limit_bytes=mib * 1024 * 1024)


def cost(flops, moved):
    return pl.CostEstimate(flops=flops, bytes_accessed=moved, transcendentals=0)


def full(*shape):
    return pl.BlockSpec(shape, lambda *_: (0,) * len(shape))


def pack_kernel(rows_ref, out_ref, rows_in, head_out, rest_out, in_sem, out_sem):
    def fetch(q):
        return pltpu.make_async_copy(
            rows_ref.at[:, :, pl.ds(q * COLS, COLS)], rows_in.at[q], in_sem.at[q]
        )

    def put(q):
        return pltpu.make_async_copy(
            head_out.at[q], out_ref.at[:, pl.ds(q * HEAD, HEAD), :], out_sem.at[q]
        )

    for q in range(PARTS):
        fetch(q).start()
    heads, rests = EXP * HEAD, EXP * REST * PARTS
    to, fr = iota((heads, heads), 0), iota((heads, heads), 1)
    move = jnp.where((to % HEAD) * EXP + to // HEAD == fr, 1.0, 0.0).astype(BF)
    to, fr = iota((rests, rests), 0), iota((rests, rests), 1)
    per = REST * PARTS
    place = (to % per) * EXP + to // per
    move_rest = jnp.where(place == fr, 1.0, 0.0).astype(BF)
    rest = []
    for q in range(PARTS):
        fetch(q).wait()
        block = rows_in[q].reshape(CAP * EXP, COLS)
        head = dot(move, block[: HEAD * EXP])
        head_out[q] = head.astype(BF).reshape(EXP, HEAD, COLS)
        put(q).start()
        rest.append(block[HEAD * EXP :])
    rest = dot(move_rest, jnp.concatenate(rest, axis=0))
    rest_out[...] = rest.astype(BF).reshape(EXP, per, COLS)
    last = pltpu.make_async_copy(
        rest_out, out_ref.at[:, pl.ds(PARTS * HEAD, per), :], out_sem.at[PARTS]
    )
    last.start()
    for q in range(PARTS):
        put(q).wait()
    last.wait()


def pack(rows):
    return pl.pallas_call(
        pack_kernel,
        out_shape=jax.ShapeDtypeStruct((EXP, CHUNK, COLS), BF),
        in_specs=[pl.BlockSpec(memory_space=HB)],
        out_specs=pl.BlockSpec(memory_space=HB),
        scratch_shapes=[
            VM((PARTS, CAP, EXP, COLS), BF),
            VM((PARTS, EXP, HEAD, COLS), BF),
            VM((EXP, REST * PARTS, COLS), BF),
            pltpu.SemaphoreType.DMA((PARTS,)),
            pltpu.SemaphoreType.DMA((PARTS + 1,)),
        ],
        compiler_params=params(32),
        cost_estimate=cost(2 * 512 * 512 * D, 2 * EXP * CAP * D * 2),
        name="pack_rows",
    )(rows)


def split2(x):
    hi = x.astype(BF)
    return hi, (x - hi.astype(F32)).astype(BF)


def gate_kernel(routing_ref, base_ref, dots_ref, pick_ref, rest_ref, logit_ref):
    experts = iota((EXP, TOK), 0)
    mask = jnp.zeros((EXP, TOK), F32)
    for k in range(4):
        mask = mask + jnp.where(routing_ref[k : k + 1, :] == experts, 1.0, 0.0)
    logits = base_ref[...] + routed_offset * mask
    raised = jnp.exp(logits - jnp.max(logits, axis=0, keepdims=True))
    probs = raised / jnp.sum(raised, axis=0, keepdims=True)
    chosen = probs * mask
    chosen_sum = jnp.sum(chosen, axis=0, keepdims=True)
    gate = chosen / chosen_sum
    earlier = jnp.where(iota((TOK, TOK), 0) < iota((TOK, TOK), 1), 1.0, 0.0).astype(BF)
    before = dot(mask.astype(BF), earlier)
    slot = jnp.where(mask > 0, before, -1.0)

    def spread(rows, per):
        grown = jnp.where(iota((rows, EXP), 0) // per == iota((rows, EXP), 1), 1.0, 0.0)
        return grown.astype(BF)

    heads, per = EXP * HEAD, REST * PARTS
    rests = EXP * per
    slot_b = slot.astype(BF)
    grow, grow_rest = spread(heads, HEAD), spread(rests, per)
    hit = dot(grow, slot_b) == (iota((heads, TOK), 0) % HEAD).astype(F32)
    hit_rest = dot(grow_rest, slot_b) == (iota((rests, TOK), 0) % REST + HEAD).astype(F32)
    hi, lo = split2(gate)

    def weighted(grown, hits):
        pair = [jnp.where(hits, dot(grown, part), 0.0).T for part in (hi, lo)]
        return jnp.concatenate(pair, axis=0).astype(BF)

    pick_ref[...] = weighted(grow, hit)
    rest_ref[...] = weighted(grow_rest, hit_rest)
    inner = jnp.zeros((EXP, TOK), F32)
    for r in range(CAP):
        inner = inner + jnp.where(slot == float(r), dots_ref[:, r : r + 1].astype(F32), 0.0)
    mean = jnp.sum(gate * inner, axis=0, keepdims=True)
    d_probs = mask * ((inner - mean) / chosen_sum)
    d_logits = probs * (d_probs - jnp.sum(probs * d_probs, axis=0, keepdims=True))
    one, rem = split2(d_logits)[0], d_logits
    rem = rem - one.astype(F32)
    two, three = split2(rem)
    logit_ref[...] = jnp.concatenate([one, two, three], axis=0)


def gates(routing, base, dots):
    heads, rests = EXP * HEAD, EXP * REST * PARTS
    return pl.pallas_call(
        gate_kernel,
        out_shape=(
            jax.ShapeDtypeStruct((2 * TOK, heads), BF),
            jax.ShapeDtypeStruct((2 * TOK, rests), BF),
            jax.ShapeDtypeStruct((3 * EXP, TOK), BF),
        ),
        compiler_params=params(16),
        cost_estimate=cost(10**8, 10**6),
        name="gates",
    )(routing, base, dots)


def combine_kernel(pick_ref, rest_ref, logit_ref, cot_ref, head_ref, tail_ref, w_ref, router_ref, out_ref):
    q = pl.program_id(0)
    rests = EXP * REST * PARTS
    piece = (iota((2 * TOK, rests), 1) % (REST * PARTS)) // REST
    rest = jnp.where(piece == q, rest_ref[...].astype(F32), 0.0).astype(BF)
    mixed = dot(pick_ref[...], head_ref[...].reshape(EXP * HEAD, COLS))
    mixed = mixed + dot(rest, tail_ref[...].reshape(rests, COLS))
    total = mixed[:TOK] + mixed[TOK:]
    router = router_ref[...]
    total = total + dot(logit_ref[...], jnp.concatenate([router] * 3, axis=0), 0, 0)
    total = total + dot(cot_ref[...], w_ref[...], 1, 1)
    out_ref[...] = total.astype(BF)


def combine(pick, rest, logit, cot, rows, w, router):
    heads, rests, per = EXP * HEAD, EXP * REST * PARTS, REST * PARTS
    return pl.pallas_call(
        combine_kernel,
        grid=(PARTS,),
        out_shape=jax.ShapeDtypeStruct((TOK, D), BF),
        in_specs=[
            full(2 * TOK, heads),
            full(2 * TOK, rests),
            full(3 * EXP, TOK),
            full(TOK, KC),
            pl.BlockSpec((EXP, HEAD, COLS), lambda q: (0, q, 0)),
            pl.BlockSpec((EXP, per, COLS), lambda q: (0, PARTS * HEAD // per, 0)),
            pl.BlockSpec((COLS, KC), lambda q: (q, 0)),
            pl.BlockSpec((EXP, COLS), lambda q: (0, q)),
        ],
        out_specs=pl.BlockSpec((TOK, COLS), lambda q: (0, q)),
        compiler_params=params(32),
        cost_estimate=cost(2 * 10**9, 8 * 10**6),
        name="combine",
    )(pick, rest, logit, cot, rows, rows, w, router)


def partial_kernel(core_ref, attn_ref, cot_ref, keep_ref, send_ref):
    first = core_ref[0] == 0
    grad = dot(attn_ref[...], cot_ref[...], 0, 0)
    for i in range(2):
        zero = grad[(2 * i) * DPROWS : (2 * i + 1) * DPROWS]
        one = grad[(2 * i + 1) * DPROWS : (2 * i + 2) * DPROWS]
        keep_ref[i] = jnp.where(first, zero, one).astype(BF)
        send_ref[i] = jnp.where(first, one, zero).astype(BF)


def partials(core, attn, cot):
    wide = 2 * CORES * DPROWS
    shape = jax.ShapeDtypeStruct((ZN, DPROWS, KC), BF)
    return pl.pallas_call(
        partial_kernel,
        grid_spec=pltpu.PrefetchScalarGridSpec(
            num_scalar_prefetch=1,
            grid=(ZN // 2,),
            in_specs=[
                pl.BlockSpec((TOK, wide), lambda i, c: (0, i)),
                pl.BlockSpec((TOK, KC), lambda i, c: (0, 0)),
            ],
            out_specs=[pl.BlockSpec((2, DPROWS, KC), lambda i, c: (i, 0, 0))] * 2,
        ),
        out_shape=(shape, shape),
        compiler_params=params(16),
        cost_estimate=cost(2 * TOK * D * KC, 5 * 10**6),
        name="key_partials",
    )(core, attn, cot)


HALF = DPROWS // 2


def near_kernel(place_ref, keep_ref, got_ref, own_ref, up_ref, down_ref, up2_ref, down2_ref):
    place = place_ref[0]
    for a in range(4):

        def total(rel):
            at = 4 * a + lax.rem(place + rel, 4)
            return keep_ref[at].astype(F32) + got_ref[at].astype(F32)

        own_ref[a] = total(0).astype(BF)
        up_ref[a] = total(1).astype(BF)
        down_ref[a] = total(3).astype(BF)
        far = total(2).astype(BF)
        up2_ref[a] = far[:HALF]
        down2_ref[a] = far[HALF:]


def smem():
    return pl.BlockSpec(memory_space=pltpu.SMEM)


def vmem():
    return pl.BlockSpec(memory_space=VM)


def near(place, keep, got):
    whole = jax.ShapeDtypeStruct((4, DPROWS, KC), BF)
    half = jax.ShapeDtypeStruct((4, HALF, KC), BF)
    return pl.pallas_call(
        near_kernel,
        in_specs=[smem(), vmem(), vmem()],
        out_specs=[vmem()] * 5,
        out_shape=(whole, whole, whole, half, half),
        compiler_params=params(24),
        cost_estimate=cost(10**6, 5 * 10**6),
        name="near_sums",
    )(place, keep, got)


def far_kernel(place_ref, own_ref, up_ref, down_ref, up2_ref, down2_ref, *outs):
    place = place_ref[0]
    for rel in range(4):
        at = lax.rem(place + rel, 4)
        total = own_ref[at].astype(F32) + up_ref[at].astype(F32) + down_ref[at].astype(F32)
        outs[rel][:HALF] = (total[:HALF] + up2_ref[at].astype(F32)).astype(BF)
        outs[rel][HALF:] = (total[HALF:] + down2_ref[at].astype(F32)).astype(BF)


def far(place, *given):
    return pl.pallas_call(
        far_kernel,
        in_specs=[smem()] + [vmem()] * 5,
        out_specs=[vmem()] * 4,
        out_shape=(jax.ShapeDtypeStruct((DPROWS, KC), BF),) * 4,
        compiler_params=params(16),
        cost_estimate=cost(10**6, 2 * 10**6),
        name="far_sums",
    )(place, *given)


def along_z(step):
    return [(i, ((i // CORES + step) % ZN) * CORES + i % CORES) for i in range(ZN * CORES)]


def shift(x, step):
    return lax.ppermute(x, "dp", along_z(step))


def adamw(weight, first, second, grad):
    new_first = beta_one * first + (1.0 - beta_one) * grad
    new_second = beta_two * second + (1.0 - beta_two) * grad * grad
    first_hat = new_first / (1.0 - beta_one**ADAM_STEP)
    second_hat = new_second / (1.0 - beta_two**ADAM_STEP)
    new_weight = weight - learn_rate * (
        first_hat / (jnp.sqrt(second_hat) + epsilon) + decay_rate * weight
    )
    return (new_weight, new_first, new_second)


def exchange(x):
    return lax.all_to_all(x, "expert", split_axis=0, concat_axis=0, tiled=True)


def local(
    attn_input,
    key_cot,
    routing,
    router_base,
    router_weight,
    expert_rows,
    expert_dots,
    key_weight,
    first_moment,
    second_moment,
):
    dp = lax.axis_index("dp")
    core, z = lax.rem(dp, CORES), dp // CORES
    near_place, far_place = lax.rem(z, 4)[None], (z // 4)[None]
    w = jnp.broadcast_to(key_weight.astype(BF)[None], (EXP, SUB, KC))
    inner = jnp.pad(expert_dots, ((0, 0), (0, KC - CAP)))[:, None, :]
    small = jnp.concatenate([w, inner, jnp.zeros_like(inner)], axis=1)
    small = exchange(small)
    w = small[:, :SUB].reshape(DPROWS, KC)
    dots = small[:, SUB, :CAP]
    w = lax.all_gather(w, "dp", axis=0, tiled=True)
    rows = exchange(pack(jnp.swapaxes(expert_rows, 0, 1)))
    pick, rest, logit = gates(routing.T, router_base.T, dots)
    keep, send = partials(core[None], attn_input, key_cot)
    got = lax.ppermute(send, "dp", [(i, i ^ 1) for i in range(ZN * CORES)])
    own, up, down, up2, down2 = near(near_place, keep, got)
    own, up, across, down = far(
        far_place, own, shift(up, 1), shift(down, -1), shift(up2, 2), shift(down2, -2)
    )
    up, across, down = shift(up, 4), shift(across, 8), shift(down, -4)
    summed = (
        own.astype(F32) + up.astype(F32) + across.astype(F32) + down.astype(F32)
    ).astype(BF)
    summed = exchange(summed.reshape(EXP, SUB, KC))
    key_grad = jnp.sum(summed.astype(F32), axis=0)
    updated = adamw(key_weight, first_moment, second_moment, key_grad)
    input_grad = combine(pick, rest, logit, key_cot, rows, w, router_weight.T)
    return (input_grad, *updated)


def solution(mesh):
    split = P(("dp", "expert"))
    in_specs = (split,) * 4 + (P(),) + (split,) * 5
    return jax.shard_map(
        local, mesh=mesh, in_specs=in_specs, out_specs=(split,) * 4, check_vma=False
    )
```

```python
import jax
import jax.numpy as jnp
from jax import lax
from jax.experimental import pallas as pl
from jax.experimental.pallas import tpu as pltpu
from jax.sharding import PartitionSpec as P

ADAM_STEP = 10

beta_one = 0.9
beta_two = 0.95
epsilon = 1e-08
learn_rate = 0.005
decay_rate = 0.1
routed_offset = 3.5

BF = jnp.bfloat16
F32 = jnp.float32

TOK, D, KC = 128, 3072, 512
EXP, CAP = 16, 34
HEAD = 32
REST = CAP - HEAD
PARTS = 8
COLS = D // PARTS
PER = REST * PARTS
CHUNK = PARTS * HEAD + PER
ZN, CORES, SUB = 16, 2, 6
DPROWS = EXP * SUB

LANES = 128
TILES = KC // LANES
BLOCK = SUB * TILES
FAR = 4
ROOM = 8

VM = pltpu.VMEM
HB = pl.ANY


def iota(shape, dim):
    return lax.broadcasted_iota(jnp.int32, shape, dim)


def dot(a, b, ca=1, cb=0):
    return lax.dot_general(a, b, (((ca,), (cb,)), ((), ())), preferred_element_type=F32)


def params(mib):
    return pltpu.CompilerParams(vmem_limit_bytes=mib * 1024 * 1024)


def cost(flops, moved):
    return pl.CostEstimate(flops=flops // 100, bytes_accessed=moved // 100, transcendentals=0)


def full(*shape):
    return pl.BlockSpec(shape, lambda *_: (0,) * len(shape))


def pack_kernel(rows_ref, out_ref, rows_in, head_out, rest_out, in_sem, out_sem):
    def fetch(q):
        return pltpu.make_async_copy(
            rows_ref.at[:, :, pl.ds(q * COLS, COLS)], rows_in.at[q], in_sem.at[q]
        )

    def put(q):
        return pltpu.make_async_copy(
            head_out.at[q], out_ref.at[:, pl.ds(q * HEAD, HEAD), :], out_sem.at[q]
        )

    for q in range(PARTS):
        fetch(q).start()
    heads, rests = EXP * HEAD, EXP * PER
    to, fr = iota((heads, heads), 0), iota((heads, heads), 1)
    move = jnp.where((to % HEAD) * EXP + to // HEAD == fr, 1.0, 0.0).astype(BF)
    to, fr = iota((rests, rests), 0), iota((rests, rests), 1)
    move_rest = jnp.where((to % PER) * EXP + to // PER == fr, 1.0, 0.0).astype(BF)
    rest = []
    for q in range(PARTS):
        fetch(q).wait()
        block = rows_in[q].reshape(CAP * EXP, COLS)
        head = dot(move, block[: HEAD * EXP])
        head_out[q] = head.astype(BF).reshape(EXP, HEAD, COLS)
        put(q).start()
        rest.append(block[HEAD * EXP :])
    rest = dot(move_rest, jnp.concatenate(rest, axis=0))
    rest_out[...] = rest.astype(BF).reshape(EXP, PER, COLS)
    last = pltpu.make_async_copy(
        rest_out, out_ref.at[:, pl.ds(PARTS * HEAD, PER), :], out_sem.at[PARTS]
    )
    last.start()
    for q in range(PARTS):
        put(q).wait()
    last.wait()


def pack(rows):
    return pl.pallas_call(
        pack_kernel,
        out_shape=jax.ShapeDtypeStruct((EXP, CHUNK, COLS), BF),
        in_specs=[pl.BlockSpec(memory_space=HB)],
        out_specs=pl.BlockSpec(memory_space=HB),
        scratch_shapes=[
            VM((PARTS, CAP, EXP, COLS), BF),
            VM((PARTS, EXP, HEAD, COLS), BF),
            VM((EXP, PER, COLS), BF),
            pltpu.SemaphoreType.DMA((PARTS,)),
            pltpu.SemaphoreType.DMA((PARTS + 1,)),
        ],
        compiler_params=params(32),
        cost_estimate=cost(2 * 512 * 512 * D, 2 * EXP * CAP * D * 2),
        name="pack_rows",
    )(rows)


def split2(x):
    hi = x.astype(BF)
    return hi, (x - hi.astype(F32)).astype(BF)


def gate_kernel(routing_ref, base_ref, dots_ref, pick_ref, rest_ref, logit_ref):
    experts = iota((EXP, TOK), 0)
    mask = jnp.zeros((EXP, TOK), F32)
    for k in range(4):
        mask = mask + jnp.where(routing_ref[k : k + 1, :] == experts, 1.0, 0.0)
    logits = base_ref[...] + routed_offset * mask
    raised = jnp.exp(logits - jnp.max(logits, axis=0, keepdims=True))
    probs = raised / jnp.sum(raised, axis=0, keepdims=True)
    chosen = probs * mask
    chosen_sum = jnp.sum(chosen, axis=0, keepdims=True)
    gate = chosen / chosen_sum
    earlier = jnp.where(iota((TOK, TOK), 0) < iota((TOK, TOK), 1), 1.0, 0.0).astype(BF)
    before = dot(mask.astype(BF), earlier)
    slot = jnp.where(mask > 0, before, -1.0)

    def spread(rows, per):
        grown = jnp.where(iota((rows, EXP), 0) // per == iota((rows, EXP), 1), 1.0, 0.0)
        return grown.astype(BF)

    heads, per = EXP * HEAD, REST * PARTS
    rests = EXP * per
    slot_b = slot.astype(BF)
    grow, grow_rest = spread(heads, HEAD), spread(rests, per)
    hit = dot(grow, slot_b) == (iota((heads, TOK), 0) % HEAD).astype(F32)
    hit_rest = dot(grow_rest, slot_b) == (iota((rests, TOK), 0) % REST + HEAD).astype(F32)
    hi, lo = split2(gate)

    def weighted(grown, hits):
        pair = [jnp.where(hits, dot(grown, part), 0.0).T for part in (hi, lo)]
        return jnp.concatenate(pair, axis=0).astype(BF)

    pick_ref[...] = weighted(grow, hit)
    rest_ref[...] = weighted(grow_rest, hit_rest)
    dots = dots_ref[...].astype(F32)[:, BLOCK, :CAP]
    inner = jnp.zeros((EXP, TOK), F32)
    for r in range(CAP):
        inner = inner + jnp.where(slot == float(r), dots[:, r : r + 1], 0.0)
    mean = jnp.sum(gate * inner, axis=0, keepdims=True)
    d_probs = mask * ((inner - mean) / chosen_sum)
    d_logits = probs * (d_probs - jnp.sum(probs * d_probs, axis=0, keepdims=True))
    one, rem = split2(d_logits)[0], d_logits
    rem = rem - one.astype(F32)
    two, three = split2(rem)
    logit_ref[...] = jnp.concatenate([one, two, three], axis=0)


def gates(routing, base, small):
    heads, rests = EXP * HEAD, EXP * PER
    return pl.pallas_call(
        gate_kernel,
        out_shape=(
            jax.ShapeDtypeStruct((2 * TOK, heads), BF),
            jax.ShapeDtypeStruct((2 * TOK, rests), BF),
            jax.ShapeDtypeStruct((3 * EXP, TOK), BF),
        ),
        grid=(1,),
        in_specs=[
            full(4, TOK),
            full(EXP, TOK),
            full(EXP, BLOCK + ROOM, LANES),
        ],
        out_specs=(full(2 * TOK, heads), full(2 * TOK, rests), full(3 * EXP, TOK)),
        compiler_params=params(16),
        cost_estimate=cost(10**8, 10**6),
        name="gates",
    )(routing, base, small)


def routed_kernel(pick_ref, rest_ref, logit_ref, head_ref, tail_ref, router_ref, out_ref):
    q = pl.program_id(0)
    rests = EXP * PER
    piece = (iota((2 * TOK, rests), 1) % PER) // REST
    rest = jnp.where(piece == q, rest_ref[...].astype(F32), 0.0).astype(BF)
    mixed = dot(pick_ref[...], head_ref[...].reshape(EXP * HEAD, COLS))
    mixed = mixed + dot(rest, tail_ref[...].reshape(rests, COLS))
    total = mixed[:TOK] + mixed[TOK:]
    router = router_ref[...]
    out_ref[...] = total + dot(logit_ref[...], jnp.concatenate([router] * 3, axis=0), 0, 0)


def routed(pick, rest, logit, rows, router):
    heads, rests = EXP * HEAD, EXP * PER
    return pl.pallas_call(
        routed_kernel,
        grid=(PARTS,),
        out_shape=jax.ShapeDtypeStruct((TOK, D), F32),
        in_specs=[
            full(2 * TOK, heads),
            full(2 * TOK, rests),
            full(3 * EXP, TOK),
            pl.BlockSpec((EXP, HEAD, COLS), lambda q: (0, q, 0)),
            pl.BlockSpec((EXP, PER, COLS), lambda q: (0, PARTS * HEAD // PER, 0)),
            pl.BlockSpec((EXP, COLS), lambda q: (0, q)),
        ],
        out_specs=pl.BlockSpec((TOK, COLS), lambda q: (0, q)),
        compiler_params=params(32),
        cost_estimate=cost(2 * 10**9, 6 * 10**6),
        name="routed_terms",
    )(pick, rest, logit, rows, rows, router)


WIDE = 2 * COLS


def final_kernel(part_ref, cot_ref, w_ref, out_ref):
    key_term = dot(cot_ref[...], w_ref[...], 1, 1)
    out_ref[...] = (part_ref[...] + key_term).astype(BF)


def final(part, cot, w):
    return pl.pallas_call(
        final_kernel,
        grid=(D // WIDE,),
        out_shape=jax.ShapeDtypeStruct((TOK, D), BF),
        in_specs=[
            pl.BlockSpec((TOK, WIDE), lambda q: (0, q)),
            full(TOK, KC),
            pl.BlockSpec((WIDE, KC), lambda q: (q, 0)),
        ],
        out_specs=pl.BlockSpec((TOK, WIDE), lambda q: (0, q)),
        compiler_params=params(32),
        cost_estimate=cost(4 * 10**8, 6 * 10**6),
        name="input_grad",
    )(part, cot, w)


def partial_kernel(core_ref, attn_ref, cot_ref, keep_ref, send_ref):
    first = core_ref[0] == 0
    grad = dot(attn_ref[...], cot_ref[...], 0, 0)
    for i in range(2):
        zero = grad[(2 * i) * DPROWS : (2 * i + 1) * DPROWS]
        one = grad[(2 * i + 1) * DPROWS : (2 * i + 2) * DPROWS]
        keep_ref[i] = jnp.where(first, zero, one).astype(BF)
        send_ref[i] = jnp.where(first, one, zero).astype(BF)


def partials(core, attn, cot):
    wide = 2 * CORES * DPROWS
    shape = jax.ShapeDtypeStruct((ZN, DPROWS, KC), BF)
    return pl.pallas_call(
        partial_kernel,
        grid_spec=pltpu.PrefetchScalarGridSpec(
            num_scalar_prefetch=1,
            grid=(ZN // 2,),
            in_specs=[
                pl.BlockSpec((TOK, wide), lambda i, c: (0, i)),
                pl.BlockSpec((TOK, KC), lambda i, c: (0, 0)),
            ],
            out_specs=[pl.BlockSpec((2, DPROWS, KC), lambda i, c: (i, 0, 0))] * 2,
        ),
        out_shape=(shape, shape),
        compiler_params=params(16),
        cost_estimate=cost(2 * TOK * D * KC, 5 * 10**6),
        name="key_partials",
    )(core, attn, cot)


def near_kernel(place_ref, keep_ref, got_ref, *outs):
    for rel in range(4):
        at = lax.rem(place_ref[0] + rel, 4)
        outs[rel][0] = (keep_ref[at].astype(F32) + got_ref[at].astype(F32)).astype(BF)


HALF = DPROWS // 2


def smem():
    return pl.BlockSpec(memory_space=pltpu.SMEM)


def vmem():
    return pl.BlockSpec(memory_space=VM)


def near(place, keep, got):
    return pl.pallas_call(
        near_kernel,
        grid=(FAR,),
        in_specs=[smem()] + [pl.BlockSpec((4, DPROWS, KC), lambda a: (a, 0, 0))] * 2,
        out_specs=[pl.BlockSpec((1, DPROWS, KC), lambda a: (a, 0, 0))] * 4,
        out_shape=(jax.ShapeDtypeStruct((FAR, DPROWS, KC), BF),) * 4,
        compiler_params=params(24),
        cost_estimate=cost(10**6, 5 * 10**6),
        name="near_sums",
    )(place, keep, got)


def terms_kernel(own_ref, up_ref, across_ref, down_ref, out_ref):
    size = DPROWS * TILES
    to, fr = iota((size, size), 0), iota((size, size), 1)
    inside = to % BLOCK
    place = (inside // SUB) * DPROWS + (to // BLOCK) * SUB + inside % SUB
    move = jnp.where(place == fr, 1.0, 0.0).astype(BF)
    pieces = []
    for a in range(FAR):
        total = own_ref[a].astype(F32) + up_ref[a].astype(F32)
        total = total + (across_ref[a].astype(F32) + down_ref[a].astype(F32))
        total = total.astype(BF)
        tall = [total[:, i * LANES : (i + 1) * LANES] for i in range(TILES)]
        piece = dot(move, jnp.concatenate(tall, axis=0))
        pieces.append(piece.reshape(EXP, BLOCK, LANES))
    out_ref[...] = jnp.concatenate(pieces, axis=1).astype(BF)


def near_terms(*given):
    return pl.pallas_call(
        terms_kernel,
        in_specs=[vmem()] * 4,
        out_specs=vmem(),
        out_shape=jax.ShapeDtypeStruct((EXP, FAR * BLOCK, LANES), BF),
        compiler_params=params(16),
        cost_estimate=cost(10**8, 2 * 10**6),
        name="near_terms",
    )(*given)


def far_kernel(terms_ref, out_ref):
    out_ref[...] = jnp.sum(terms_ref[...].astype(F32), axis=0)


def far_terms(terms):
    return pl.pallas_call(
        far_kernel,
        in_specs=[vmem()],
        out_specs=vmem(),
        out_shape=jax.ShapeDtypeStruct((FAR * BLOCK, LANES), F32),
        compiler_params=params(16),
        cost_estimate=cost(10**6, 10**6),
        name="far_terms",
    )(terms)


def adamw_kernel(terms_ref, weight_ref, first_ref, second_ref, *outs):
    total = jnp.sum(terms_ref[...], axis=0)
    grad = jnp.concatenate([total[i * SUB : (i + 1) * SUB] for i in range(TILES)], axis=1)
    for out, value in zip(outs, adamw(weight_ref[...], first_ref[...], second_ref[...], grad)):
        out[...] = value


def update(*given):
    return pl.pallas_call(
        adamw_kernel,
        in_specs=[vmem()] * 4,
        out_specs=[vmem()] * 3,
        out_shape=(jax.ShapeDtypeStruct((SUB, KC), F32),) * 3,
        compiler_params=params(16),
        cost_estimate=cost(10**6, 10**6),
        name="adamw",
    )(*given)


def small_kernel(weight_ref, dots_ref, out_ref):
    weight = weight_ref[...]
    tall = jnp.concatenate([weight[:, i * LANES : (i + 1) * LANES] for i in range(TILES)], axis=0)
    to, fr = iota((EXP * ROOM, EXP), 0), iota((EXP * ROOM, EXP), 1)
    spread = dot(jnp.where(to == fr * ROOM, 1.0, 0.0).astype(BF), dots_ref[...])
    spread = spread.reshape(EXP, ROOM, LANES)
    tall = jnp.broadcast_to(tall[None], (EXP, BLOCK, LANES))
    out_ref[...] = jnp.concatenate([tall, spread], axis=1).astype(BF)


def small_block(weight, dots):
    return pl.pallas_call(
        small_kernel,
        in_specs=[vmem()] * 2,
        out_specs=vmem(),
        out_shape=jax.ShapeDtypeStruct((EXP, BLOCK + ROOM, LANES), BF),
        compiler_params=params(16),
        cost_estimate=cost(10**6, 10**6),
        name="small_block",
    )(weight, dots)


def order_kernel(small_ref, out_ref):
    size = EXP * (BLOCK + ROOM)
    blocks = small_ref[...].reshape(size, LANES)
    fr = iota((1, size), 1)
    expert, inside = fr // (BLOCK + ROOM), fr % (BLOCK + ROOM)
    row = expert * SUB + inside % SUB
    to = iota((DPROWS, size), 0)
    for i in range(TILES):
        move = jnp.where(jnp.where(inside // SUB == i, row, -1) == to, 1.0, 0.0).astype(BF)
        out_ref[:, i * LANES : (i + 1) * LANES] = dot(move, blocks).astype(BF)


def order_rows(small):
    return pl.pallas_call(
        order_kernel,
        in_specs=[vmem()],
        out_specs=vmem(),
        out_shape=jax.ShapeDtypeStruct((DPROWS, KC), BF),
        compiler_params=params(16),
        cost_estimate=cost(10**8, 10**6),
        name="order_key_rows",
    )(small)


def along_z(step):
    return [(i, ((i // CORES + step) % ZN) * CORES + i % CORES) for i in range(ZN * CORES)]


def shift(x, step):
    return lax.ppermute(x, "dp", along_z(step))


def adamw(weight, first, second, grad):
    new_first = beta_one * first + (1.0 - beta_one) * grad
    new_second = beta_two * second + (1.0 - beta_two) * grad * grad
    first_hat = new_first / (1.0 - beta_one**ADAM_STEP)
    second_hat = new_second / (1.0 - beta_two**ADAM_STEP)
    new_weight = weight - learn_rate * (
        first_hat / (jnp.sqrt(second_hat) + epsilon) + decay_rate * weight
    )
    return (new_weight, new_first, new_second)


def exchange(x):
    return lax.all_to_all(x, "expert", split_axis=0, concat_axis=0, tiled=True)


def exchange_far(x):
    groups = [
        [(4 * a + b) * CORES + c for a in range(FAR)] for b in range(4) for c in range(CORES)
    ]
    return lax.all_to_all(x, "dp", 0, 0, axis_index_groups=groups, tiled=True)


def swap_core(x):
    return lax.ppermute(x, "dp", [(i, i ^ 1) for i in range(ZN * CORES)])


def local(
    attn_input,
    key_cot,
    routing,
    router_base,
    router_weight,
    expert_rows,
    expert_dots,
    key_weight,
    first_moment,
    second_moment,
):
    dp = lax.axis_index("dp")
    core, z = lax.rem(dp, CORES)[None], dp // CORES
    near_place = lax.rem(z, 4)[None]
    dots = jnp.pad(expert_dots, ((0, 0), (0, LANES - CAP)))
    small, cot = lax.optimization_barrier((small_block(key_weight, dots), key_cot))
    small = exchange(small)
    keep, send = partials(core, attn_input, cot)
    got = swap_core(send)
    packed = pack(jnp.swapaxes(expert_rows, 0, 1))
    small, packed, keep, got = lax.optimization_barrier((small, packed, keep, got))
    key_rows, packed, keep = lax.optimization_barrier((order_rows(small), packed, keep))
    w = lax.all_gather(key_rows, "dp", axis=0, tiled=True)
    rows = exchange(packed)
    own, up, across, down = near(near_place, keep, got)
    terms = near_terms(own, shift(up, 1), shift(across, -2), shift(down, -1))
    terms, rows = lax.optimization_barrier((terms, rows))
    grads = far_terms(exchange(terms))
    pick, rest, logit = gates(routing.T, router_base.T, small)
    part = routed(pick, rest, logit, rows, router_weight.T)
    grads = exchange_far(grads.reshape(FAR, BLOCK, LANES))
    updated = update(grads, key_weight, first_moment, second_moment)
    input_grad = final(part, key_cot, w)
    return (input_grad, *updated)


def solution(mesh):
    split = P(("dp", "expert"))
    in_specs = (split,) * 4 + (P(),) + (split,) * 5
    return jax.shard_map(
        local, mesh=mesh, in_specs=in_specs, out_specs=(split,) * 4, check_vma=False
    )
```

```python
import jax
import jax.numpy as jnp
from jax import lax
from jax.experimental import pallas as pl
from jax.experimental.pallas import tpu as pltpu
from jax.sharding import PartitionSpec as P

ADAM_STEP = 10

beta_one = 0.9
beta_two = 0.95
epsilon = 1e-08
learn_rate = 0.005
decay_rate = 0.1
routed_offset = 3.5

BF = jnp.bfloat16
F32 = jnp.float32

TOK, D, KC = 128, 3072, 512
EXP, CAP = 16, 34
HEAD = 32
REST = CAP - HEAD
PARTS = 8
COLS = D // PARTS
PER = REST * PARTS
ROWS = PARTS * HEAD + PER
ZN, CORES, SUB = 16, 2, 6
DPROWS = EXP * SUB

LANES = 128
TILES = KC // LANES
BLOCK = SUB * TILES
FAR = 4
SPAN = COLS // LANES
LINE = BLOCK // SPAN
KEYS = ZN * LINE
ROOM = 8

VM = pltpu.VMEM
HB = pl.ANY


def iota(shape, dim):
    return lax.broadcasted_iota(jnp.int32, shape, dim)


def dot(a, b, ca=1, cb=0):
    return lax.dot_general(a, b, (((ca,), (cb,)), ((), ())), preferred_element_type=F32)


def params(mib):
    return pltpu.CompilerParams(vmem_limit_bytes=mib * 1024 * 1024)


def cost(flops, moved):
    return pl.CostEstimate(flops=flops // 100, bytes_accessed=moved // 100, transcendentals=0)


BIG = 56


def smem():
    return pl.BlockSpec(memory_space=pltpu.SMEM)


def full(*shape):
    return pl.BlockSpec(shape, lambda *_: (0,) * len(shape))


def pack_kernel(rows_ref, out_ref, rows_in, head_out, rest_out, in_sem, out_sem):
    def fetch(q):
        return pltpu.make_async_copy(
            rows_ref.at[:, :, pl.ds(q * COLS, COLS)], rows_in.at[q], in_sem.at[q]
        )

    def put(q):
        return pltpu.make_async_copy(
            head_out.at[q], out_ref.at[:, pl.ds(q * HEAD, HEAD), :], out_sem.at[q]
        )

    for q in range(PARTS):
        fetch(q).start()
    heads, rests = EXP * HEAD, EXP * PER
    to, fr = iota((heads, heads), 0), iota((heads, heads), 1)
    move = jnp.where((to % HEAD) * EXP + to // HEAD == fr, 1.0, 0.0).astype(BF)
    to, fr = iota((rests, rests), 0), iota((rests, rests), 1)
    move_rest = jnp.where((to % PER) * EXP + to // PER == fr, 1.0, 0.0).astype(BF)
    rest = []
    for q in range(PARTS):
        fetch(q).wait()
        block = rows_in[q].reshape(CAP * EXP, COLS)
        head = dot(move, block[: HEAD * EXP])
        head_out[q] = head.astype(BF).reshape(EXP, HEAD, COLS)
        put(q).start()
        rest.append(block[HEAD * EXP :])
    rest = dot(move_rest, jnp.concatenate(rest, axis=0))
    rest_out[...] = rest.astype(BF).reshape(EXP, PER, COLS)
    last = pltpu.make_async_copy(
        rest_out, out_ref.at[:, pl.ds(PARTS * HEAD, PER), :], out_sem.at[PARTS]
    )
    last.start()
    for q in range(PARTS):
        put(q).wait()
    last.wait()


def pack(rows):
    return pl.pallas_call(
        pack_kernel,
        out_shape=jax.ShapeDtypeStruct((EXP, ROWS, COLS), BF),
        in_specs=[pl.BlockSpec(memory_space=HB)],
        out_specs=pl.BlockSpec(memory_space=HB),
        scratch_shapes=[
            VM((PARTS, CAP, EXP, COLS), BF),
            VM((PARTS, EXP, HEAD, COLS), BF),
            VM((EXP, PER, COLS), BF),
            pltpu.SemaphoreType.DMA((PARTS,)),
            pltpu.SemaphoreType.DMA((PARTS + 1,)),
        ],
        compiler_params=params(BIG),
        cost_estimate=cost(2 * 512 * 512 * D, 2 * EXP * CAP * D * 2),
        name="pack_rows",
    )(rows)


def split2(x):
    hi = x.astype(BF)
    return hi, (x - hi.astype(F32)).astype(BF)


def gate_kernel(routing_ref, base_ref, dots_ref, pick_ref, rest_ref, logit_ref):
    experts = iota((EXP, TOK), 0)
    mask = jnp.zeros((EXP, TOK), F32)
    for k in range(4):
        mask = mask + jnp.where(routing_ref[k : k + 1, :] == experts, 1.0, 0.0)
    logits = base_ref[...] + routed_offset * mask
    raised = jnp.exp(logits - jnp.max(logits, axis=0, keepdims=True))
    probs = raised / jnp.sum(raised, axis=0, keepdims=True)
    chosen = probs * mask
    chosen_sum = jnp.sum(chosen, axis=0, keepdims=True)
    gate = chosen / chosen_sum
    earlier = jnp.where(iota((TOK, TOK), 0) < iota((TOK, TOK), 1), 1.0, 0.0).astype(BF)
    before = dot(mask.astype(BF), earlier)
    slot = jnp.where(mask > 0, before, -1.0)

    def spread(rows, per):
        grown = jnp.where(iota((rows, EXP), 0) // per == iota((rows, EXP), 1), 1.0, 0.0)
        return grown.astype(BF)

    heads, per = EXP * HEAD, REST * PARTS
    rests = EXP * per
    slot_b = slot.astype(BF)
    grow, grow_rest = spread(heads, HEAD), spread(rests, per)
    hit = dot(grow, slot_b) == (iota((heads, TOK), 0) % HEAD).astype(F32)
    hit_rest = dot(grow_rest, slot_b) == (iota((rests, TOK), 0) % REST + HEAD).astype(F32)
    hi, lo = split2(gate)

    def weighted(grown, hits):
        pair = [jnp.where(hits, dot(grown, part), 0.0).T for part in (hi, lo)]
        return jnp.concatenate(pair, axis=0).astype(BF)

    pick_ref[...] = weighted(grow, hit)
    rest_ref[...] = weighted(grow_rest, hit_rest)
    dots = dots_ref[...].astype(F32)[:, BLOCK, :CAP]
    inner = jnp.zeros((EXP, TOK), F32)
    for r in range(CAP):
        inner = inner + jnp.where(slot == float(r), dots[:, r : r + 1], 0.0)
    mean = jnp.sum(gate * inner, axis=0, keepdims=True)
    d_probs = mask * ((inner - mean) / chosen_sum)
    d_logits = probs * (d_probs - jnp.sum(probs * d_probs, axis=0, keepdims=True))
    one, rem = split2(d_logits)[0], d_logits
    rem = rem - one.astype(F32)
    two, three = split2(rem)
    logit_ref[...] = jnp.concatenate([one, two, three], axis=0)


def gates(routing, base, small):
    heads, rests = EXP * HEAD, EXP * PER
    return pl.pallas_call(
        gate_kernel,
        out_shape=(
            jax.ShapeDtypeStruct((2 * TOK, heads), BF),
            jax.ShapeDtypeStruct((2 * TOK, rests), BF),
            jax.ShapeDtypeStruct((3 * EXP, TOK), BF),
        ),
        grid=(1,),
        in_specs=[
            full(4, TOK),
            full(EXP, TOK),
            full(EXP, BLOCK + ROOM, LANES),
        ],
        out_specs=(full(2 * TOK, heads), full(2 * TOK, rests), full(3 * EXP, TOK)),
        compiler_params=params(16),
        cost_estimate=cost(10**8, 10**6),
        name="gates",
    )(routing, base, small)


def combine_kernel(
    pick_ref, rest_ref, logit_ref, cot_ref, head_ref, tail_ref, w_ref, router_ref, out_ref
):
    q = pl.program_id(0)
    rests = EXP * PER
    piece = (iota((2 * TOK, rests), 1) % PER) // REST
    rest = jnp.where(piece == q, rest_ref[...].astype(F32), 0.0).astype(BF)
    mixed = dot(pick_ref[...], head_ref[...].reshape(EXP * HEAD, COLS))
    mixed = mixed + dot(rest, tail_ref[...].reshape(rests, COLS))
    total = mixed[:TOK] + mixed[TOK:]
    router = router_ref[...]
    total = total + dot(logit_ref[...], jnp.concatenate([router] * 3, axis=0), 0, 0)
    total = total + dot(cot_ref[...], w_ref[...], 1, 1)
    out_ref[...] = total.astype(BF)


def combine(pick, rest, logit, cot, rows, w, router):
    heads, rests = EXP * HEAD, EXP * PER
    return pl.pallas_call(
        combine_kernel,
        grid=(PARTS,),
        out_shape=jax.ShapeDtypeStruct((TOK, D), BF),
        in_specs=[
            full(2 * TOK, heads),
            full(2 * TOK, rests),
            full(3 * EXP, TOK),
            full(TOK, KC),
            pl.BlockSpec((EXP, HEAD, COLS), lambda q: (0, q, 0)),
            pl.BlockSpec((EXP, PER, COLS), lambda q: (0, PARTS * HEAD // PER, 0)),
            pl.BlockSpec((COLS, KC), lambda q: (q, 0)),
            pl.BlockSpec((EXP, COLS), lambda q: (0, q)),
        ],
        out_specs=pl.BlockSpec((TOK, COLS), lambda q: (0, q)),
        compiler_params=params(BIG),
        cost_estimate=cost(2 * 10**9, 8 * 10**6),
        name="combine",
    )(pick, rest, logit, cot, rows, rows, w, router)


def partial_kernel(core_ref, attn_ref, cot_ref, keep_ref, send_ref):
    first = core_ref[0] == 0
    grad = dot(attn_ref[...], cot_ref[...], 0, 0)
    for i in range(2):
        zero = grad[(2 * i) * DPROWS : (2 * i + 1) * DPROWS]
        one = grad[(2 * i + 1) * DPROWS : (2 * i + 2) * DPROWS]
        keep_ref[i] = jnp.where(first, zero, one).astype(BF)
        send_ref[i] = jnp.where(first, one, zero).astype(BF)


def partials(core, attn, cot):
    wide = 2 * CORES * DPROWS
    shape = jax.ShapeDtypeStruct((ZN, DPROWS, KC), BF)
    return pl.pallas_call(
        partial_kernel,
        grid_spec=pltpu.PrefetchScalarGridSpec(
            num_scalar_prefetch=1,
            grid=(ZN // 2,),
            in_specs=[
                pl.BlockSpec((TOK, wide), lambda i, c: (0, i)),
                pl.BlockSpec((TOK, KC), lambda i, c: (0, 0)),
            ],
            out_specs=[pl.BlockSpec((2, DPROWS, KC), lambda i, c: (i, 0, 0))] * 2,
        ),
        out_shape=(shape, shape),
        compiler_params=params(16),
        cost_estimate=cost(2 * TOK * D * KC, 5 * 10**6),
        name="key_partials",
    )(core, attn, cot)


PIECES = [
    (tile, span)
    for tile in range(TILES)
    for span in range(SPAN)
    if tile * SUB < (span + 1) * LINE and (tile + 1) * SUB > span * LINE
]


def fill_kernel(keep_ref, got_ref, out_ref, moves):
    tall, wide = 2 * EXP * LINE, 2 * DPROWS

    @pl.when(pl.program_id(0) == 0)
    def _():
        to, fr = iota((tall, wide), 0), iota((tall, wide), 1)
        expert, pair, line = to // (2 * LINE), (to // LINE) % 2, to % LINE
        same = (fr // DPROWS == pair) & ((fr % DPROWS) // SUB == expert)
        for n, (tile, span) in enumerate(PIECES):
            hit = same & (tile * SUB + fr % SUB == span * LINE + line)
            moves[n] = jnp.where(hit, 1.0, 0.0).astype(BF)

    for i in range(2):
        at = slice(2 * i, 2 * i + 2)
        total = keep_ref[at].astype(F32) + got_ref[at].astype(F32)
        total = total.reshape(wide, KC).astype(BF)
        spans = [jnp.zeros((tall, LANES), F32)] * SPAN
        for n, (tile, span) in enumerate(PIECES):
            spans[span] = spans[span] + dot(moves[n], total[:, tile * LANES : (tile + 1) * LANES])
        out = jnp.concatenate(spans, axis=1).astype(BF)
        out_ref[:, i * 2 * LINE : (i + 1) * 2 * LINE, :] = out.reshape(EXP, 2 * LINE, COLS)


def fill(keep, got):
    block = pl.BlockSpec((4, DPROWS, KC), lambda i: (i, 0, 0))
    return pl.pallas_call(
        fill_kernel,
        grid=(ZN // 4,),
        out_shape=jax.ShapeDtypeStruct((EXP, KEYS, COLS), BF),
        in_specs=[block, block],
        out_specs=pl.BlockSpec((EXP, 4 * LINE, COLS), lambda i: (0, i, 0)),
        scratch_shapes=[VM((len(PIECES), 2 * EXP * LINE, 2 * DPROWS), BF)],
        compiler_params=params(16),
        cost_estimate=cost(10**6, 2 * 10**6),
        name="fill_key_terms",
    )(keep, got)


def near_kernel(place_ref, terms_ref, *refs):
    *outs, total_ref = refs
    total = jnp.sum(terms_ref[...].astype(F32), axis=0)
    total_ref[...] = total.reshape(ZN, LINE, COLS)
    for rel in range(4):
        for a in range(FAR):
            outs[rel][a] = total_ref[4 * a + lax.rem(place_ref[0] + rel, 4)]


def near_terms(place, terms):
    return pl.pallas_call(
        near_kernel,
        in_specs=[smem(), vmem()],
        out_specs=[vmem()] * 4,
        out_shape=(jax.ShapeDtypeStruct((FAR, LINE, COLS), F32),) * 4,
        scratch_shapes=[VM((ZN, LINE, COLS), F32)],
        compiler_params=params(16),
        cost_estimate=cost(10**6, 2 * 10**6),
        name="near_terms",
    )(place, terms)


def far_kernel(place_ref, own_ref, up_ref, across_ref, down_ref, *outs):
    for rel in range(FAR):
        at = lax.rem(place_ref[0] + rel, FAR)
        outs[rel][...] = own_ref[at] + up_ref[at] + (across_ref[at] + down_ref[at])


def far_terms(place, *given):
    return pl.pallas_call(
        far_kernel,
        in_specs=[smem()] + [vmem()] * 4,
        out_specs=[vmem()] * 4,
        out_shape=(jax.ShapeDtypeStruct((LINE, COLS), F32),) * 4,
        compiler_params=params(16),
        cost_estimate=cost(10**6, 10**6),
        name="far_terms",
    )(place, *given)


def vmem():
    return pl.BlockSpec(memory_space=VM)


def adamw_kernel(own_ref, up_ref, across_ref, down_ref, weight_ref, first_ref, second_ref, *outs):
    total = own_ref[...] + up_ref[...] + (across_ref[...] + down_ref[...])
    total = [total[:, i * LANES : (i + 1) * LANES] for i in range(SPAN)]
    total = jnp.concatenate(total, axis=0)
    grad = jnp.concatenate([total[i * SUB : (i + 1) * SUB] for i in range(TILES)], axis=1)
    for out, value in zip(outs, adamw(weight_ref[...], first_ref[...], second_ref[...], grad)):
        out[...] = value


def update(*given):
    return pl.pallas_call(
        adamw_kernel,
        in_specs=[vmem()] * 7,
        out_specs=[vmem()] * 3,
        out_shape=(jax.ShapeDtypeStruct((SUB, KC), F32),) * 3,
        compiler_params=params(16),
        cost_estimate=cost(10**6, 10**6),
        name="adamw",
    )(*given)


def small_kernel(weight_ref, dots_ref, out_ref):
    weight = weight_ref[...]
    tall = jnp.concatenate([weight[:, i * LANES : (i + 1) * LANES] for i in range(TILES)], axis=0)
    to, fr = iota((EXP * ROOM, EXP), 0), iota((EXP * ROOM, EXP), 1)
    dots = jnp.concatenate([dots_ref[...], jnp.zeros((EXP, LANES - CAP), BF)], axis=1)
    spread = dot(jnp.where(to == fr * ROOM, 1.0, 0.0).astype(BF), dots)
    spread = spread.reshape(EXP, ROOM, LANES)
    tall = jnp.broadcast_to(tall[None], (EXP, BLOCK, LANES))
    out_ref[...] = jnp.concatenate([tall, spread], axis=1).astype(BF)


def small_block(weight, dots):
    return pl.pallas_call(
        small_kernel,
        in_specs=[vmem()] * 2,
        out_specs=vmem(),
        out_shape=jax.ShapeDtypeStruct((EXP, BLOCK + ROOM, LANES), BF),
        compiler_params=params(16),
        cost_estimate=cost(10**6, 10**6),
        name="small_block",
    )(weight, dots)


def order_kernel(small_ref, out_ref):
    size = EXP * (BLOCK + ROOM)
    blocks = small_ref[...].reshape(size, LANES)
    fr = iota((1, size), 1)
    expert, inside = fr // (BLOCK + ROOM), fr % (BLOCK + ROOM)
    row = expert * SUB + inside % SUB
    to = iota((DPROWS, size), 0)
    for i in range(TILES):
        move = jnp.where(jnp.where(inside // SUB == i, row, -1) == to, 1.0, 0.0).astype(BF)
        out_ref[:, i * LANES : (i + 1) * LANES] = dot(move, blocks).astype(BF)


def order_rows(small):
    return pl.pallas_call(
        order_kernel,
        in_specs=[vmem()],
        out_specs=vmem(),
        out_shape=jax.ShapeDtypeStruct((DPROWS, KC), BF),
        compiler_params=params(16),
        cost_estimate=cost(10**8, 10**6),
        name="order_key_rows",
    )(small)


def adamw(weight, first, second, grad):
    new_first = beta_one * first + (1.0 - beta_one) * grad
    new_second = beta_two * second + (1.0 - beta_two) * grad * grad
    first_hat = new_first / (1.0 - beta_one**ADAM_STEP)
    second_hat = new_second / (1.0 - beta_two**ADAM_STEP)
    new_weight = weight - learn_rate * (
        first_hat / (jnp.sqrt(second_hat) + epsilon) + decay_rate * weight
    )
    return (new_weight, new_first, new_second)


def exchange(x):
    return lax.all_to_all(x, "expert", split_axis=0, concat_axis=0, tiled=True)


def shift(x, step):
    pairs = [(i, ((i // CORES + step) % ZN) * CORES + i % CORES) for i in range(ZN * CORES)]
    return lax.ppermute(x, "dp", pairs)


def swap_core(x):
    return lax.ppermute(x, "dp", [(i, i ^ 1) for i in range(ZN * CORES)])


def local(
    attn_input,
    key_cot,
    routing,
    router_base,
    router_weight,
    expert_rows,
    expert_dots,
    key_weight,
    first_moment,
    second_moment,
):
    dp = lax.axis_index("dp")
    core, z = lax.rem(dp, CORES)[None], dp // CORES
    near_place, far_place = lax.rem(z, 4)[None], (z // 4)[None]
    small, cot = lax.optimization_barrier((small_block(key_weight, expert_dots), key_cot))
    small = exchange(small)
    keep, send = partials(core, attn_input, cot)
    terms = fill(keep, swap_core(send))
    small, terms = lax.optimization_barrier((small, terms))
    w = lax.all_gather(order_rows(small), "dp", axis=0, tiled=True)
    terms, own_rows = lax.optimization_barrier((terms, expert_rows))
    terms = exchange(terms)
    packed = pack(jnp.swapaxes(own_rows, 0, 1))
    terms, packed = lax.optimization_barrier((terms, packed))
    rows = exchange(packed)
    own, up, across, down = near_terms(near_place, terms)
    own, up, across, down = far_terms(
        far_place, own, shift(up, 1), shift(across, -2), shift(down, -1)
    )
    grads = own, shift(up, 4), shift(across, 8), shift(down, -4)
    updated = update(*grads, key_weight, first_moment, second_moment)
    pick, rest, logit = gates(routing.T, router_base.T, small)
    rows, pick, updated = lax.optimization_barrier((rows, pick, updated))
    input_grad = combine(pick, rest, logit, key_cot, rows, w, router_weight.T)
    return (input_grad, *updated)


def solution(mesh):
    split = P(("dp", "expert"))
    in_specs = (split,) * 4 + (P(),) + (split,) * 5
    return jax.shard_map(
        local, mesh=mesh, in_specs=in_specs, out_specs=(split,) * 4, check_vma=False
    )
```

```python
import jax
import jax.numpy as jnp
from jax import lax
from jax.experimental import pallas as pl
from jax.experimental.pallas import tpu as pltpu
from jax.sharding import PartitionSpec as P

ADAM_STEP = 10

beta_one = 0.9
beta_two = 0.95
epsilon = 1e-08
learn_rate = 0.005
decay_rate = 0.1
routed_offset = 3.5

BF = jnp.bfloat16
F32 = jnp.float32

TOK, D, KC = 128, 3072, 512
EXP, CAP = 16, 34
HEAD = 32
REST = CAP - HEAD
PARTS = 8
COLS = D // PARTS
PER = REST * PARTS
ROWS = PARTS * HEAD + PER
ZN, CORES, SUB = 16, 2, 6
DPROWS = EXP * SUB

LANES = 128
TILES = KC // LANES
BLOCK = SUB * TILES
FAR = 4
SPAN = COLS // LANES
LINE = BLOCK // SPAN
KEYS = ZN * LINE
ROOM = 8

VM = pltpu.VMEM
HB = pl.ANY


def iota(shape, dim):
    return lax.broadcasted_iota(jnp.int32, shape, dim)


def dot(a, b, ca=1, cb=0):
    return lax.dot_general(a, b, (((ca,), (cb,)), ((), ())), preferred_element_type=F32)


def params(mib):
    return pltpu.CompilerParams(vmem_limit_bytes=mib * 1024 * 1024)


def cost(flops, moved):
    return pl.CostEstimate(flops=flops // 100, bytes_accessed=moved // 100, transcendentals=0)


BIG = 56


def smem():
    return pl.BlockSpec(memory_space=pltpu.SMEM)


def full(*shape):
    return pl.BlockSpec(shape, lambda *_: (0,) * len(shape))


def pack_kernel(rows_ref, out_ref, rows_in, head_out, rest_out, in_sem, out_sem):
    def fetch(q):
        return pltpu.make_async_copy(
            rows_ref.at[:, :, pl.ds(q * COLS, COLS)], rows_in.at[q], in_sem.at[q]
        )

    def put(q):
        return pltpu.make_async_copy(
            head_out.at[q], out_ref.at[:, pl.ds(q * HEAD, HEAD), :], out_sem.at[q]
        )

    for q in range(PARTS):
        fetch(q).start()
    heads, rests = EXP * HEAD, EXP * PER
    to, fr = iota((heads, heads), 0), iota((heads, heads), 1)
    move = jnp.where((to % HEAD) * EXP + to // HEAD == fr, 1.0, 0.0).astype(BF)
    to, fr = iota((rests, rests), 0), iota((rests, rests), 1)
    move_rest = jnp.where((to % PER) * EXP + to // PER == fr, 1.0, 0.0).astype(BF)
    rest = []
    for q in range(PARTS):
        fetch(q).wait()
        block = rows_in[q].reshape(CAP * EXP, COLS)
        head = dot(move, block[: HEAD * EXP])
        head_out[q] = head.astype(BF).reshape(EXP, HEAD, COLS)
        put(q).start()
        rest.append(block[HEAD * EXP :])
    rest = dot(move_rest, jnp.concatenate(rest, axis=0))
    rest_out[...] = rest.astype(BF).reshape(EXP, PER, COLS)
    last = pltpu.make_async_copy(
        rest_out, out_ref.at[:, pl.ds(PARTS * HEAD, PER), :], out_sem.at[PARTS]
    )
    last.start()
    for q in range(PARTS):
        put(q).wait()
    last.wait()


def pack(rows):
    return pl.pallas_call(
        pack_kernel,
        out_shape=jax.ShapeDtypeStruct((EXP, ROWS, COLS), BF),
        in_specs=[pl.BlockSpec(memory_space=HB)],
        out_specs=pl.BlockSpec(memory_space=HB),
        scratch_shapes=[
            VM((PARTS, CAP, EXP, COLS), BF),
            VM((PARTS, EXP, HEAD, COLS), BF),
            VM((EXP, PER, COLS), BF),
            pltpu.SemaphoreType.DMA((PARTS,)),
            pltpu.SemaphoreType.DMA((PARTS + 1,)),
        ],
        compiler_params=params(BIG),
        cost_estimate=cost(2 * 512 * 512 * D, 2 * EXP * CAP * D * 2),
        name="pack_rows",
    )(rows)


def split2(x):
    hi = x.astype(BF)
    return hi, (x - hi.astype(F32)).astype(BF)


def gate_kernel(routing_ref, base_ref, dots_ref, pick_ref, rest_ref, logit_ref):
    experts = iota((EXP, TOK), 0)
    mask = jnp.zeros((EXP, TOK), F32)
    for k in range(4):
        mask = mask + jnp.where(routing_ref[k : k + 1, :] == experts, 1.0, 0.0)
    logits = base_ref[...] + routed_offset * mask
    raised = jnp.exp(logits - jnp.max(logits, axis=0, keepdims=True))
    probs = raised / jnp.sum(raised, axis=0, keepdims=True)
    chosen = probs * mask
    chosen_sum = jnp.sum(chosen, axis=0, keepdims=True)
    gate = chosen / chosen_sum
    earlier = jnp.where(iota((TOK, TOK), 0) < iota((TOK, TOK), 1), 1.0, 0.0).astype(BF)
    before = dot(mask.astype(BF), earlier)
    slot = jnp.where(mask > 0, before, -1.0)

    def spread(rows, per):
        grown = jnp.where(iota((rows, EXP), 0) // per == iota((rows, EXP), 1), 1.0, 0.0)
        return grown.astype(BF)

    heads, per = EXP * HEAD, REST * PARTS
    rests = EXP * per
    slot_b = slot.astype(BF)
    grow, grow_rest = spread(heads, HEAD), spread(rests, per)
    hit = dot(grow, slot_b) == (iota((heads, TOK), 0) % HEAD).astype(F32)
    hit_rest = dot(grow_rest, slot_b) == (iota((rests, TOK), 0) % REST + HEAD).astype(F32)
    hi, lo = split2(gate)

    def weighted(grown, hits):
        pair = [jnp.where(hits, dot(grown, part), 0.0).T for part in (hi, lo)]
        return jnp.concatenate(pair, axis=0).astype(BF)

    pick_ref[...] = weighted(grow, hit)
    rest_ref[...] = weighted(grow_rest, hit_rest)
    dots = dots_ref[...].astype(F32)[:, BLOCK, :CAP]
    inner = jnp.zeros((EXP, TOK), F32)
    for r in range(CAP):
        inner = inner + jnp.where(slot == float(r), dots[:, r : r + 1], 0.0)
    mean = jnp.sum(gate * inner, axis=0, keepdims=True)
    d_probs = mask * ((inner - mean) / chosen_sum)
    d_logits = probs * (d_probs - jnp.sum(probs * d_probs, axis=0, keepdims=True))
    one, rem = split2(d_logits)[0], d_logits
    rem = rem - one.astype(F32)
    two, three = split2(rem)
    logit_ref[...] = jnp.concatenate([one, two, three], axis=0)


def gates(routing, base, small):
    heads, rests = EXP * HEAD, EXP * PER
    return pl.pallas_call(
        gate_kernel,
        out_shape=(
            jax.ShapeDtypeStruct((2 * TOK, heads), BF),
            jax.ShapeDtypeStruct((2 * TOK, rests), BF),
            jax.ShapeDtypeStruct((3 * EXP, TOK), BF),
        ),
        grid=(1,),
        in_specs=[
            full(4, TOK),
            full(EXP, TOK),
            full(EXP, BLOCK + ROOM, LANES),
        ],
        out_specs=(full(2 * TOK, heads), full(2 * TOK, rests), full(3 * EXP, TOK)),
        compiler_params=params(16),
        cost_estimate=cost(10**8, 10**6),
        name="gates",
    )(routing, base, small)


STEP = 2


def combine_kernel(
    pick_ref, rest_ref, logit_ref, cot_ref, head_ref, tail_ref, w_ref, router_ref, out_ref
):
    rests = EXP * PER
    piece = (iota((2 * TOK, rests), 1) % PER) // REST
    picked = rest_ref[...].astype(F32)
    tail = tail_ref[...].reshape(rests, COLS)
    router = jnp.concatenate([router_ref[...]] * 3, axis=0)
    total = dot(cot_ref[...], w_ref[...], 1, 1) + dot(logit_ref[...], router, 0, 0)
    for i in range(STEP):
        q = pl.program_id(0) * STEP + i
        rest = jnp.where(piece == q, picked, 0.0).astype(BF)
        head = head_ref[:, i * HEAD : (i + 1) * HEAD, :].reshape(EXP * HEAD, COLS)
        mixed = dot(pick_ref[...], head) + dot(rest, tail)
        at = slice(i * COLS, (i + 1) * COLS)
        out_ref[:, at] = (total[:, at] + mixed[:TOK] + mixed[TOK:]).astype(BF)


def combine(pick, rest, logit, cot, rows, w, router):
    heads, rests, wide = EXP * HEAD, EXP * PER, STEP * COLS
    return pl.pallas_call(
        combine_kernel,
        grid=(PARTS // STEP,),
        out_shape=jax.ShapeDtypeStruct((TOK, D), BF),
        in_specs=[
            full(2 * TOK, heads),
            full(2 * TOK, rests),
            full(3 * EXP, TOK),
            full(TOK, KC),
            pl.BlockSpec((EXP, STEP * HEAD, COLS), lambda q: (0, q, 0)),
            pl.BlockSpec((EXP, PER, COLS), lambda q: (0, PARTS * HEAD // PER, 0)),
            pl.BlockSpec((wide, KC), lambda q: (q, 0)),
            pl.BlockSpec((EXP, wide), lambda q: (0, q)),
        ],
        out_specs=pl.BlockSpec((TOK, wide), lambda q: (0, q)),
        compiler_params=params(BIG),
        cost_estimate=cost(2 * 10**9, 8 * 10**6),
        name="combine",
    )(pick, rest, logit, cot, rows, rows, w, router)


PIECES = [
    (tile, span)
    for tile in range(TILES)
    for span in range(SPAN)
    if tile * SUB < (span + 1) * LINE and (tile + 1) * SUB > span * LINE
]


def terms_kernel(core_ref, attn_ref, attn2_ref, cot_ref, cot2_ref, out_ref, moves):
    tall, wide = 2 * EXP * LINE, 2 * DPROWS

    @pl.when(pl.program_id(0) == 0)
    def _():
        to, fr = iota((tall, wide), 0), iota((tall, wide), 1)
        expert, pair, line = to // (2 * LINE), (to // LINE) % 2, to % LINE
        same = (fr // DPROWS == pair) & ((fr % DPROWS) // SUB == expert)
        for n, (tile, span) in enumerate(PIECES):
            hit = same & (tile * SUB + fr % SUB == span * LINE + line)
            moves[n] = jnp.where(hit, 1.0, 0.0).astype(BF)

    first = core_ref[0] == 0
    attn = jnp.concatenate([attn_ref[...], attn2_ref[...]], axis=0)
    cot = jnp.concatenate([cot_ref[...], cot2_ref[...]], axis=0)
    grad = dot(attn, cot, 0, 0)
    for i in range(2):
        total = []
        for j in (2 * i, 2 * i + 1):
            zero = grad[2 * j * DPROWS : (2 * j + 1) * DPROWS]
            one = grad[(2 * j + 1) * DPROWS : (2 * j + 2) * DPROWS]
            total.append(jnp.where(first, zero, one))
        total = jnp.concatenate(total, axis=0).astype(BF)
        spans = [jnp.zeros((tall, LANES), F32)] * SPAN
        for n, (tile, span) in enumerate(PIECES):
            spans[span] = spans[span] + dot(moves[n], total[:, tile * LANES : (tile + 1) * LANES])
        out = jnp.concatenate(spans, axis=1).astype(BF)
        out_ref[:, i * 2 * LINE : (i + 1) * 2 * LINE, :] = out.reshape(EXP, 2 * LINE, COLS)


def key_terms(core, attn, attn2, cot, cot2):
    columns = pl.BlockSpec((TOK, 4 * CORES * DPROWS), lambda i: (0, i))
    return pl.pallas_call(
        terms_kernel,
        grid=(ZN // 4,),
        out_shape=jax.ShapeDtypeStruct((EXP, KEYS, COLS), BF),
        in_specs=[smem(), columns, columns, full(TOK, KC), full(TOK, KC)],
        out_specs=pl.BlockSpec((EXP, 4 * LINE, COLS), lambda i: (0, i, 0)),
        scratch_shapes=[VM((len(PIECES), 2 * EXP * LINE, 2 * DPROWS), BF)],
        compiler_params=params(BIG),
        cost_estimate=cost(10**6, 2 * 10**6),
        name="key_terms",
    )(core, attn, attn2, cot, cot2)


def near_kernel(place_ref, terms_ref, *refs):
    *outs, total_ref = refs
    total = jnp.sum(terms_ref[...].astype(F32), axis=0)
    total_ref[...] = total.reshape(ZN, LINE, COLS)
    for rel in range(4):
        for a in range(FAR):
            outs[rel][a] = total_ref[4 * a + lax.rem(place_ref[0] + rel, 4)]


def near_terms(place, terms):
    return pl.pallas_call(
        near_kernel,
        in_specs=[smem(), vmem()],
        out_specs=[vmem()] * 4,
        out_shape=(jax.ShapeDtypeStruct((FAR, LINE, COLS), F32),) * 4,
        scratch_shapes=[VM((ZN, LINE, COLS), F32)],
        compiler_params=params(16),
        cost_estimate=cost(10**6, 2 * 10**6),
        name="near_terms",
    )(place, terms)


def far_kernel(place_ref, own_ref, up_ref, across_ref, down_ref, *outs):
    for rel in range(FAR):
        at = lax.rem(place_ref[0] + rel, FAR)
        outs[rel][...] = own_ref[at] + up_ref[at] + (across_ref[at] + down_ref[at])


def far_terms(place, *given):
    return pl.pallas_call(
        far_kernel,
        in_specs=[smem()] + [vmem()] * 4,
        out_specs=[vmem()] * 4,
        out_shape=(jax.ShapeDtypeStruct((LINE, COLS), F32),) * 4,
        compiler_params=params(16),
        cost_estimate=cost(10**6, 10**6),
        name="far_terms",
    )(place, *given)


def vmem():
    return pl.BlockSpec(memory_space=VM)


def adamw_kernel(own_ref, up_ref, across_ref, down_ref, weight_ref, first_ref, second_ref, *outs):
    total = own_ref[...] + up_ref[...] + (across_ref[...] + down_ref[...])
    total = [total[:, i * LANES : (i + 1) * LANES] for i in range(SPAN)]
    total = jnp.concatenate(total, axis=0)
    grad = jnp.concatenate([total[i * SUB : (i + 1) * SUB] for i in range(TILES)], axis=1)
    for out, value in zip(outs, adamw(weight_ref[...], first_ref[...], second_ref[...], grad)):
        out[...] = value


def update(*given):
    return pl.pallas_call(
        adamw_kernel,
        in_specs=[vmem()] * 7,
        out_specs=[vmem()] * 3,
        out_shape=(jax.ShapeDtypeStruct((SUB, KC), F32),) * 3,
        compiler_params=params(16),
        cost_estimate=cost(10**6, 10**6),
        name="adamw",
    )(*given)


def small_kernel(weight_ref, dots_ref, out_ref):
    weight = weight_ref[...]
    tall = jnp.concatenate([weight[:, i * LANES : (i + 1) * LANES] for i in range(TILES)], axis=0)
    to, fr = iota((EXP * ROOM, EXP), 0), iota((EXP * ROOM, EXP), 1)
    dots = jnp.concatenate([dots_ref[...], jnp.zeros((EXP, LANES - CAP), BF)], axis=1)
    spread = dot(jnp.where(to == fr * ROOM, 1.0, 0.0).astype(BF), dots)
    spread = spread.reshape(EXP, ROOM, LANES)
    tall = jnp.broadcast_to(tall[None], (EXP, BLOCK, LANES))
    out_ref[...] = jnp.concatenate([tall, spread], axis=1).astype(BF)


def small_block(weight, dots):
    return pl.pallas_call(
        small_kernel,
        in_specs=[vmem()] * 2,
        out_specs=vmem(),
        out_shape=jax.ShapeDtypeStruct((EXP, BLOCK + ROOM, LANES), BF),
        compiler_params=params(BIG),
        cost_estimate=cost(10**6, 10**6),
        name="small_block",
    )(weight, dots)


def order_kernel(small_ref, out_ref):
    size = EXP * (BLOCK + ROOM)
    blocks = small_ref[...].reshape(size, LANES)
    fr = iota((1, size), 1)
    expert, inside = fr // (BLOCK + ROOM), fr % (BLOCK + ROOM)
    row = expert * SUB + inside % SUB
    to = iota((DPROWS, size), 0)
    for i in range(TILES):
        move = jnp.where(jnp.where(inside // SUB == i, row, -1) == to, 1.0, 0.0).astype(BF)
        out_ref[:, i * LANES : (i + 1) * LANES] = dot(move, blocks).astype(BF)


def order_rows(small):
    return pl.pallas_call(
        order_kernel,
        in_specs=[vmem()],
        out_specs=vmem(),
        out_shape=jax.ShapeDtypeStruct((DPROWS, KC), BF),
        compiler_params=params(16),
        cost_estimate=cost(10**8, 10**6),
        name="order_key_rows",
    )(small)


def adamw(weight, first, second, grad):
    new_first = beta_one * first + (1.0 - beta_one) * grad
    new_second = beta_two * second + (1.0 - beta_two) * grad * grad
    first_hat = new_first / (1.0 - beta_one**ADAM_STEP)
    second_hat = new_second / (1.0 - beta_two**ADAM_STEP)
    new_weight = weight - learn_rate * (
        first_hat / (jnp.sqrt(second_hat) + epsilon) + decay_rate * weight
    )
    return (new_weight, new_first, new_second)


def exchange(x):
    return lax.all_to_all(x, "expert", split_axis=0, concat_axis=0, tiled=True)


def shift(x, step):
    pairs = [(i, ((i // CORES + step) % ZN) * CORES + i % CORES) for i in range(ZN * CORES)]
    return lax.ppermute(x, "dp", pairs)


def swap_core(x):
    return lax.ppermute(x, "dp", [(i, i ^ 1) for i in range(ZN * CORES)])


def local(
    attn_input,
    key_cot,
    routing,
    router_base,
    router_weight,
    expert_rows,
    expert_dots,
    key_weight,
    first_moment,
    second_moment,
):
    dp = lax.axis_index("dp")
    core, z = lax.rem(dp, CORES)[None], dp // CORES
    near_place, far_place = lax.rem(z, 4)[None], (z // 4)[None]
    small = exchange(small_block(key_weight, expert_dots))
    terms = key_terms(core, attn_input, swap_core(attn_input), key_cot, swap_core(key_cot))
    small, terms = lax.optimization_barrier((small, terms))
    w = lax.all_gather(order_rows(small), "dp", axis=0, tiled=True)
    terms, own_rows = lax.optimization_barrier((terms, expert_rows))
    terms = exchange(terms)
    packed = pack(jnp.swapaxes(own_rows, 0, 1))
    terms, packed = lax.optimization_barrier((terms, packed))
    rows = exchange(packed)
    own, up, across, down = near_terms(near_place, terms)
    own, up, across, down = far_terms(
        far_place, own, shift(up, 1), shift(across, -2), shift(down, -1)
    )
    grads = own, shift(up, 4), shift(across, 8), shift(down, -4)
    updated = update(*grads, key_weight, first_moment, second_moment)
    pick, rest, logit = gates(routing.T, router_base.T, small)
    rows, pick, updated = lax.optimization_barrier((rows, pick, updated))
    input_grad = combine(pick, rest, logit, key_cot, rows, w, router_weight.T)
    return (input_grad, *updated)


def solution(mesh):
    split = P(("dp", "expert"))
    in_specs = (split,) * 4 + (P(),) + (split,) * 5
    return jax.shard_map(
        local, mesh=mesh, in_specs=in_specs, out_specs=(split,) * 4, check_vma=False
    )
```

```python
import jax
import jax.numpy as jnp
from jax import lax
from jax.experimental import pallas as pl
from jax.experimental.pallas import tpu as pltpu
from jax.sharding import PartitionSpec as P

ADAM_STEP = 10

beta_one = 0.9
beta_two = 0.95
epsilon = 1e-08
learn_rate = 0.005
decay_rate = 0.1
routed_offset = 3.5

BF = jnp.bfloat16
F32 = jnp.float32

TOK, D, KC = 128, 3072, 512
EXP, CAP = 16, 34
HEAD = 32
REST = CAP - HEAD
PARTS = 8
COLS = D // PARTS
PER = REST * PARTS
ROWS = PARTS * HEAD + PER
ZN, CORES, SUB = 16, 2, 6
DPROWS = EXP * SUB

LANES = 128
TILES = KC // LANES
BLOCK = SUB * TILES
FAR = 4
SPAN = COLS // LANES
LINE = BLOCK // SPAN
KEYS = ZN * LINE
ROOM = 8

VM = pltpu.VMEM
HB = pl.ANY


def iota(shape, dim):
    return lax.broadcasted_iota(jnp.int32, shape, dim)


def dot(a, b, ca=1, cb=0):
    return lax.dot_general(a, b, (((ca,), (cb,)), ((), ())), preferred_element_type=F32)


def params(mib):
    return pltpu.CompilerParams(vmem_limit_bytes=mib * 1024 * 1024)


def cost(flops, moved):
    return pl.CostEstimate(flops=flops // 100, bytes_accessed=moved // 100, transcendentals=0)


BIG = 56


def smem():
    return pl.BlockSpec(memory_space=pltpu.SMEM)


def full(*shape):
    return pl.BlockSpec(shape, lambda *_: (0,) * len(shape))


def pack_kernel(rows_ref, out_ref, rows_in, head_out, rest_out, in_sem, out_sem):
    def fetch(q):
        return pltpu.make_async_copy(
            rows_ref.at[:, :, pl.ds(q * COLS, COLS)], rows_in.at[q], in_sem.at[q]
        )

    def put(q):
        return pltpu.make_async_copy(
            head_out.at[q], out_ref.at[:, pl.ds(q * HEAD, HEAD), :], out_sem.at[q]
        )

    for q in range(PARTS):
        fetch(q).start()
    heads, rests = EXP * HEAD, EXP * PER
    to, fr = iota((heads, heads), 0), iota((heads, heads), 1)
    move = jnp.where((to % HEAD) * EXP + to // HEAD == fr, 1.0, 0.0).astype(BF)
    to, fr = iota((rests, rests), 0), iota((rests, rests), 1)
    move_rest = jnp.where((to % PER) * EXP + to // PER == fr, 1.0, 0.0).astype(BF)
    rest = []
    for q in range(PARTS):
        fetch(q).wait()
        block = rows_in[q].reshape(CAP * EXP, COLS)
        head = dot(move, block[: HEAD * EXP])
        head_out[q] = head.astype(BF).reshape(EXP, HEAD, COLS)
        put(q).start()
        rest.append(block[HEAD * EXP :])
    rest = dot(move_rest, jnp.concatenate(rest, axis=0))
    rest_out[...] = rest.astype(BF).reshape(EXP, PER, COLS)
    last = pltpu.make_async_copy(
        rest_out, out_ref.at[:, pl.ds(PARTS * HEAD, PER), :], out_sem.at[PARTS]
    )
    last.start()
    for q in range(PARTS):
        put(q).wait()
    last.wait()


def pack(rows):
    return pl.pallas_call(
        pack_kernel,
        out_shape=jax.ShapeDtypeStruct((EXP, ROWS, COLS), BF),
        in_specs=[pl.BlockSpec(memory_space=HB)],
        out_specs=pl.BlockSpec(memory_space=HB),
        scratch_shapes=[
            VM((PARTS, CAP, EXP, COLS), BF),
            VM((PARTS, EXP, HEAD, COLS), BF),
            VM((EXP, PER, COLS), BF),
            pltpu.SemaphoreType.DMA((PARTS,)),
            pltpu.SemaphoreType.DMA((PARTS + 1,)),
        ],
        compiler_params=params(BIG),
        cost_estimate=cost(2 * 512 * 512 * D, 2 * EXP * CAP * D * 2),
        name="pack_rows",
    )(rows)


def split2(x):
    hi = x.astype(BF)
    return hi, (x - hi.astype(F32)).astype(BF)


def gate_kernel(routing_ref, base_ref, dots_ref, pick_ref, rest_ref, logit_ref):
    experts = iota((EXP, TOK), 0)
    mask = jnp.zeros((EXP, TOK), F32)
    for k in range(4):
        mask = mask + jnp.where(routing_ref[k : k + 1, :] == experts, 1.0, 0.0)
    logits = base_ref[...] + routed_offset * mask
    raised = jnp.exp(logits - jnp.max(logits, axis=0, keepdims=True))
    probs = raised / jnp.sum(raised, axis=0, keepdims=True)
    chosen = probs * mask
    chosen_sum = jnp.sum(chosen, axis=0, keepdims=True)
    gate = chosen / chosen_sum
    earlier = jnp.where(iota((TOK, TOK), 0) < iota((TOK, TOK), 1), 1.0, 0.0).astype(BF)
    before = dot(mask.astype(BF), earlier)
    slot = jnp.where(mask > 0, before, -1.0)

    def spread(rows, per):
        grown = jnp.where(iota((rows, EXP), 0) // per == iota((rows, EXP), 1), 1.0, 0.0)
        return grown.astype(BF)

    heads, per = EXP * HEAD, REST * PARTS
    rests = EXP * per
    slot_b = slot.astype(BF)
    grow, grow_rest = spread(heads, HEAD), spread(rests, per)
    hit = dot(grow, slot_b) == (iota((heads, TOK), 0) % HEAD).astype(F32)
    hit_rest = dot(grow_rest, slot_b) == (iota((rests, TOK), 0) % REST + HEAD).astype(F32)
    hi, lo = split2(gate)

    def weighted(grown, hits):
        pair = [jnp.where(hits, dot(grown, part), 0.0).T for part in (hi, lo)]
        return jnp.concatenate(pair, axis=0).astype(BF)

    pick_ref[...] = weighted(grow, hit)
    rest_ref[...] = weighted(grow_rest, hit_rest)
    dots = dots_ref[...].astype(F32)[:, BLOCK, :CAP]
    inner = jnp.zeros((EXP, TOK), F32)
    for r in range(CAP):
        inner = inner + jnp.where(slot == float(r), dots[:, r : r + 1], 0.0)
    mean = jnp.sum(gate * inner, axis=0, keepdims=True)
    d_probs = mask * ((inner - mean) / chosen_sum)
    d_logits = probs * (d_probs - jnp.sum(probs * d_probs, axis=0, keepdims=True))
    one, rem = split2(d_logits)[0], d_logits
    rem = rem - one.astype(F32)
    two, three = split2(rem)
    logit_ref[...] = jnp.concatenate([one, two, three], axis=0)


def gates(routing, base, small):
    heads, rests = EXP * HEAD, EXP * PER
    return pl.pallas_call(
        gate_kernel,
        out_shape=(
            jax.ShapeDtypeStruct((2 * TOK, heads), BF),
            jax.ShapeDtypeStruct((2 * TOK, rests), BF),
            jax.ShapeDtypeStruct((3 * EXP, TOK), BF),
        ),
        grid=(1,),
        in_specs=[
            full(4, TOK),
            full(EXP, TOK),
            full(EXP, BLOCK + ROOM, LANES),
        ],
        out_specs=(full(2 * TOK, heads), full(2 * TOK, rests), full(3 * EXP, TOK)),
        compiler_params=params(16),
        cost_estimate=cost(10**8, 10**6),
        name="gates",
    )(routing, base, small)


STEP = 4


def combine_kernel(
    pick_ref, rest_ref, logit_ref, cot_ref, head_ref, tail_ref, w_ref, router_ref, out_ref
):
    rests = EXP * PER
    piece = (iota((2 * TOK, rests), 1) % PER) // REST
    picked = rest_ref[...].astype(F32)
    tail = tail_ref[...].reshape(rests, COLS)
    router = jnp.concatenate([router_ref[...]] * 3, axis=0)
    total = dot(cot_ref[...], w_ref[...], 1, 1) + dot(logit_ref[...], router, 0, 0)
    for i in range(STEP):
        q = pl.program_id(0) * STEP + i
        rest = jnp.where(piece == q, picked, 0.0).astype(BF)
        head = head_ref[:, i * HEAD : (i + 1) * HEAD, :].reshape(EXP * HEAD, COLS)
        mixed = dot(pick_ref[...], head) + dot(rest, tail)
        at = slice(i * COLS, (i + 1) * COLS)
        out_ref[:, at] = (total[:, at] + mixed[:TOK] + mixed[TOK:]).astype(BF)


def combine(pick, rest, logit, cot, rows, w, router):
    heads, rests, wide = EXP * HEAD, EXP * PER, STEP * COLS
    return pl.pallas_call(
        combine_kernel,
        grid=(PARTS // STEP,),
        out_shape=jax.ShapeDtypeStruct((TOK, D), BF),
        in_specs=[
            full(2 * TOK, heads),
            full(2 * TOK, rests),
            full(3 * EXP, TOK),
            full(TOK, KC),
            pl.BlockSpec((EXP, STEP * HEAD, COLS), lambda q: (0, q, 0)),
            pl.BlockSpec((EXP, PER, COLS), lambda q: (0, PARTS * HEAD // PER, 0)),
            pl.BlockSpec((wide, KC), lambda q: (q, 0)),
            pl.BlockSpec((EXP, wide), lambda q: (0, q)),
        ],
        out_specs=pl.BlockSpec((TOK, wide), lambda q: (0, q)),
        compiler_params=params(BIG),
        cost_estimate=cost(2 * 10**9, 8 * 10**6),
        name="combine",
    )(pick, rest, logit, cot, rows, rows, w, router)


PIECES = [
    (tile, span)
    for tile in range(TILES)
    for span in range(SPAN)
    if tile * SUB < (span + 1) * LINE and (tile + 1) * SUB > span * LINE
]


def terms_kernel(core_ref, attn_ref, attn2_ref, cot_ref, cot2_ref, out_ref, moves):
    tall, wide = 2 * EXP * LINE, 2 * DPROWS

    @pl.when(pl.program_id(0) == 0)
    def _():
        to, fr = iota((tall, wide), 0), iota((tall, wide), 1)
        expert, pair, line = to // (2 * LINE), (to // LINE) % 2, to % LINE
        same = (fr // DPROWS == pair) & ((fr % DPROWS) // SUB == expert)
        for n, (tile, span) in enumerate(PIECES):
            hit = same & (tile * SUB + fr % SUB == span * LINE + line)
            moves[n] = jnp.where(hit, 1.0, 0.0).astype(BF)

    first = core_ref[0] == 0
    attn = jnp.concatenate([attn_ref[...], attn2_ref[...]], axis=0)
    cot = jnp.concatenate([cot_ref[...], cot2_ref[...]], axis=0)
    grad = dot(attn, cot, 0, 0)
    kept = []
    for j in range(4):
        zero = grad[2 * j * DPROWS : (2 * j + 1) * DPROWS]
        one = grad[(2 * j + 1) * DPROWS : (2 * j + 2) * DPROWS]
        kept.append(jnp.where(first, zero, one).astype(BF))
    pairs = [jnp.concatenate(kept[2 * i : 2 * i + 2], axis=0) for i in range(2)]
    spans = [jnp.zeros((tall, 2 * LANES), F32)] * SPAN
    for n, (tile, span) in enumerate(PIECES):
        at = slice(tile * LANES, (tile + 1) * LANES)
        both = jnp.concatenate([pair[:, at] for pair in pairs], axis=1)
        spans[span] = spans[span] + dot(moves[n], both)
    for i in range(2):
        at = slice(i * LANES, (i + 1) * LANES)
        out = jnp.concatenate([span[:, at] for span in spans], axis=1).astype(BF)
        out_ref[:, i * 2 * LINE : (i + 1) * 2 * LINE, :] = out.reshape(EXP, 2 * LINE, COLS)


def key_terms(core, attn, attn2, cot, cot2):
    columns = pl.BlockSpec((TOK, 4 * CORES * DPROWS), lambda i: (0, i))
    return pl.pallas_call(
        terms_kernel,
        grid=(ZN // 4,),
        out_shape=jax.ShapeDtypeStruct((EXP, KEYS, COLS), BF),
        in_specs=[smem(), columns, columns, full(TOK, KC), full(TOK, KC)],
        out_specs=pl.BlockSpec((EXP, 4 * LINE, COLS), lambda i: (0, i, 0)),
        scratch_shapes=[VM((len(PIECES), 2 * EXP * LINE, 2 * DPROWS), BF)],
        compiler_params=params(BIG),
        cost_estimate=cost(10**6, 2 * 10**6),
        name="key_terms",
    )(core, attn, attn2, cot, cot2)


def near_kernel(place_ref, terms_ref, *refs):
    *outs, total_ref = refs
    total = jnp.sum(terms_ref[...].astype(F32), axis=0)
    total_ref[...] = total.reshape(ZN, LINE, COLS)
    for rel in range(4):
        for a in range(FAR):
            outs[rel][a] = total_ref[4 * a + lax.rem(place_ref[0] + rel, 4)]


def near_terms(place, terms):
    return pl.pallas_call(
        near_kernel,
        in_specs=[smem(), vmem()],
        out_specs=[vmem()] * 4,
        out_shape=(jax.ShapeDtypeStruct((FAR, LINE, COLS), F32),) * 4,
        scratch_shapes=[VM((ZN, LINE, COLS), F32)],
        compiler_params=params(16),
        cost_estimate=cost(10**6, 2 * 10**6),
        name="near_terms",
    )(place, terms)


def far_kernel(place_ref, own_ref, up_ref, across_ref, down_ref, *outs):
    for rel in range(FAR):
        at = lax.rem(place_ref[0] + rel, FAR)
        outs[rel][...] = own_ref[at] + up_ref[at] + (across_ref[at] + down_ref[at])


def far_terms(place, *given):
    return pl.pallas_call(
        far_kernel,
        in_specs=[smem()] + [vmem()] * 4,
        out_specs=[vmem()] * 4,
        out_shape=(jax.ShapeDtypeStruct((LINE, COLS), F32),) * 4,
        compiler_params=params(16),
        cost_estimate=cost(10**6, 10**6),
        name="far_terms",
    )(place, *given)


def vmem():
    return pl.BlockSpec(memory_space=VM)


def adamw_kernel(own_ref, up_ref, across_ref, down_ref, weight_ref, first_ref, second_ref, *outs):
    total = own_ref[...] + up_ref[...] + (across_ref[...] + down_ref[...])
    total = [total[:, i * LANES : (i + 1) * LANES] for i in range(SPAN)]
    total = jnp.concatenate(total, axis=0)
    grad = jnp.concatenate([total[i * SUB : (i + 1) * SUB] for i in range(TILES)], axis=1)
    for out, value in zip(outs, adamw(weight_ref[...], first_ref[...], second_ref[...], grad)):
        out[...] = value


def update(*given):
    return pl.pallas_call(
        adamw_kernel,
        in_specs=[vmem()] * 7,
        out_specs=[vmem()] * 3,
        out_shape=(jax.ShapeDtypeStruct((SUB, KC), F32),) * 3,
        compiler_params=params(16),
        cost_estimate=cost(10**6, 10**6),
        name="adamw",
    )(*given)


def small_kernel(weight_ref, dots_ref, out_ref):
    weight = weight_ref[...]
    tall = jnp.concatenate([weight[:, i * LANES : (i + 1) * LANES] for i in range(TILES)], axis=0)
    to, fr = iota((EXP * ROOM, EXP), 0), iota((EXP * ROOM, EXP), 1)
    dots = jnp.concatenate([dots_ref[...], jnp.zeros((EXP, LANES - CAP), BF)], axis=1)
    spread = dot(jnp.where(to == fr * ROOM, 1.0, 0.0).astype(BF), dots)
    spread = spread.reshape(EXP, ROOM, LANES)
    tall = jnp.broadcast_to(tall[None], (EXP, BLOCK, LANES))
    out_ref[...] = jnp.concatenate([tall, spread], axis=1).astype(BF)


def small_block(weight, dots):
    return pl.pallas_call(
        small_kernel,
        in_specs=[vmem()] * 2,
        out_specs=vmem(),
        out_shape=jax.ShapeDtypeStruct((EXP, BLOCK + ROOM, LANES), BF),
        compiler_params=params(BIG),
        cost_estimate=cost(10**6, 10**6),
        name="small_block",
    )(weight, dots)


def order_kernel(small_ref, out_ref):
    size = EXP * (BLOCK + ROOM)
    blocks = small_ref[...].reshape(size, LANES)
    fr = iota((1, size), 1)
    expert, inside = fr // (BLOCK + ROOM), fr % (BLOCK + ROOM)
    row = expert * SUB + inside % SUB
    to = iota((DPROWS, size), 0)
    for i in range(TILES):
        move = jnp.where(jnp.where(inside // SUB == i, row, -1) == to, 1.0, 0.0).astype(BF)
        out_ref[:, i * LANES : (i + 1) * LANES] = dot(move, blocks).astype(BF)


def order_rows(small):
    return pl.pallas_call(
        order_kernel,
        in_specs=[vmem()],
        out_specs=vmem(),
        out_shape=jax.ShapeDtypeStruct((DPROWS, KC), BF),
        compiler_params=params(16),
        cost_estimate=cost(10**8, 10**6),
        name="order_key_rows",
    )(small)


def adamw(weight, first, second, grad):
    new_first = beta_one * first + (1.0 - beta_one) * grad
    new_second = beta_two * second + (1.0 - beta_two) * grad * grad
    first_hat = new_first / (1.0 - beta_one**ADAM_STEP)
    second_hat = new_second / (1.0 - beta_two**ADAM_STEP)
    new_weight = weight - learn_rate * (
        first_hat / (jnp.sqrt(second_hat) + epsilon) + decay_rate * weight
    )
    return (new_weight, new_first, new_second)


def exchange(x):
    return lax.all_to_all(x, "expert", split_axis=0, concat_axis=0, tiled=True)


def shift(x, step):
    pairs = [(i, ((i // CORES + step) % ZN) * CORES + i % CORES) for i in range(ZN * CORES)]
    return lax.ppermute(x, "dp", pairs)


def swap_core(x):
    return lax.ppermute(x, "dp", [(i, i ^ 1) for i in range(ZN * CORES)])


def local(
    attn_input,
    key_cot,
    routing,
    router_base,
    router_weight,
    expert_rows,
    expert_dots,
    key_weight,
    first_moment,
    second_moment,
):
    dp = lax.axis_index("dp")
    core, z = lax.rem(dp, CORES)[None], dp // CORES
    near_place, far_place = lax.rem(z, 4)[None], (z // 4)[None]
    small = exchange(small_block(key_weight, expert_dots))
    terms = key_terms(core, attn_input, swap_core(attn_input), key_cot, swap_core(key_cot))
    small, terms = lax.optimization_barrier((small, terms))
    w = lax.all_gather(order_rows(small), "dp", axis=0, tiled=True)
    terms, own_rows = lax.optimization_barrier((terms, expert_rows))
    terms = exchange(terms)
    packed = pack(jnp.swapaxes(own_rows, 0, 1))
    terms, packed = lax.optimization_barrier((terms, packed))
    rows = exchange(packed)
    own, up, across, down = near_terms(near_place, terms)
    own, up, across, down = far_terms(
        far_place, own, shift(up, 1), shift(across, -2), shift(down, -1)
    )
    grads = own, shift(up, 4), shift(across, 8), shift(down, -4)
    updated = update(*grads, key_weight, first_moment, second_moment)
    pick, rest, logit = gates(routing.T, router_base.T, small)
    rows, pick, updated = lax.optimization_barrier((rows, pick, updated))
    input_grad = combine(pick, rest, logit, key_cot, rows, w, router_weight.T)
    return (input_grad, *updated)


def solution(mesh):
    split = P(("dp", "expert"))
    in_specs = (split,) * 4 + (P(),) + (split,) * 5
    return jax.shard_map(
        local, mesh=mesh, in_specs=in_specs, out_specs=(split,) * 4, check_vma=False
    )
```

```python
import jax
import jax.numpy as jnp
from jax import lax
from jax.experimental import pallas as pl
from jax.experimental.pallas import tpu as pltpu
from jax.sharding import PartitionSpec as P

ADAM_STEP = 10

beta_one = 0.9
beta_two = 0.95
epsilon = 1e-08
learn_rate = 0.005
decay_rate = 0.1
routed_offset = 3.5

BF = jnp.bfloat16
F32 = jnp.float32

TOK, D, KC = 128, 3072, 512
EXP, CAP = 16, 34
HEAD = 32
REST = CAP - HEAD
PARTS = 8
COLS = D // PARTS
PER = REST * PARTS
ROWS = PARTS * HEAD + PER
ZN, CORES, SUB = 16, 2, 6
DPROWS = EXP * SUB

LANES = 128
TILES = KC // LANES
BLOCK = SUB * TILES
FAR = 4
SPAN = COLS // LANES
LINE = BLOCK // SPAN
KEYS = ZN * LINE
ROOM = 8

VM = pltpu.VMEM
HB = pl.ANY


def iota(shape, dim):
    return lax.broadcasted_iota(jnp.int32, shape, dim)


def dot(a, b, ca=1, cb=0):
    return lax.dot_general(a, b, (((ca,), (cb,)), ((), ())), preferred_element_type=F32)


def params(mib):
    return pltpu.CompilerParams(vmem_limit_bytes=mib * 1024 * 1024)


def cost(flops, moved):
    return pl.CostEstimate(flops=flops // 100, bytes_accessed=moved // 100, transcendentals=0)


BIG = 56


def smem():
    return pl.BlockSpec(memory_space=pltpu.SMEM)


def full(*shape):
    return pl.BlockSpec(shape, lambda *_: (0,) * len(shape))


def pack_kernel(rows_ref, out_ref, rows_in, head_out, rest_out, in_sem, out_sem):
    def fetch(q):
        return pltpu.make_async_copy(
            rows_ref.at[:, :, pl.ds(q * COLS, COLS)], rows_in.at[q], in_sem.at[q]
        )

    def put(q):
        return pltpu.make_async_copy(
            head_out.at[q], out_ref.at[:, pl.ds(q * HEAD, HEAD), :], out_sem.at[q]
        )

    for q in range(PARTS):
        fetch(q).start()
    heads, rests = EXP * HEAD, EXP * PER
    to, fr = iota((heads, heads), 0), iota((heads, heads), 1)
    move = jnp.where((to % HEAD) * EXP + to // HEAD == fr, 1.0, 0.0).astype(BF)
    to, fr = iota((rests, rests), 0), iota((rests, rests), 1)
    move_rest = jnp.where((to % PER) * EXP + to // PER == fr, 1.0, 0.0).astype(BF)
    rest = []
    for q in range(PARTS):
        fetch(q).wait()
        block = rows_in[q].reshape(CAP * EXP, COLS)
        head = dot(move, block[: HEAD * EXP])
        head_out[q] = head.astype(BF).reshape(EXP, HEAD, COLS)
        put(q).start()
        rest.append(block[HEAD * EXP :])
    rest = dot(move_rest, jnp.concatenate(rest, axis=0))
    rest_out[...] = rest.astype(BF).reshape(EXP, PER, COLS)
    last = pltpu.make_async_copy(
        rest_out, out_ref.at[:, pl.ds(PARTS * HEAD, PER), :], out_sem.at[PARTS]
    )
    last.start()
    for q in range(PARTS):
        put(q).wait()
    last.wait()


def pack(rows):
    return pl.pallas_call(
        pack_kernel,
        out_shape=jax.ShapeDtypeStruct((EXP, ROWS, COLS), BF),
        in_specs=[pl.BlockSpec(memory_space=HB)],
        out_specs=pl.BlockSpec(memory_space=HB),
        scratch_shapes=[
            VM((PARTS, CAP, EXP, COLS), BF),
            VM((PARTS, EXP, HEAD, COLS), BF),
            VM((EXP, PER, COLS), BF),
            pltpu.SemaphoreType.DMA((PARTS,)),
            pltpu.SemaphoreType.DMA((PARTS + 1,)),
        ],
        compiler_params=params(BIG),
        cost_estimate=cost(2 * 512 * 512 * D, 2 * EXP * CAP * D * 2),
        name="pack_rows",
    )(rows)


def split2(x):
    hi = x.astype(BF)
    return hi, (x - hi.astype(F32)).astype(BF)


def gate_kernel(routing_ref, base_ref, dots_ref, pick_ref, rest_ref, logit_ref):
    experts = iota((EXP, TOK), 0)
    mask = jnp.zeros((EXP, TOK), F32)
    for k in range(4):
        mask = mask + jnp.where(routing_ref[k : k + 1, :] == experts, 1.0, 0.0)
    logits = base_ref[...] + routed_offset * mask
    raised = jnp.exp(logits - jnp.max(logits, axis=0, keepdims=True))
    probs = raised / jnp.sum(raised, axis=0, keepdims=True)
    chosen = probs * mask
    chosen_sum = jnp.sum(chosen, axis=0, keepdims=True)
    gate = chosen / chosen_sum
    earlier = jnp.where(iota((TOK, TOK), 0) < iota((TOK, TOK), 1), 1.0, 0.0).astype(BF)
    before = dot(mask.astype(BF), earlier)
    slot = jnp.where(mask > 0, before, -1.0)

    def spread(rows, per):
        grown = jnp.where(iota((rows, EXP), 0) // per == iota((rows, EXP), 1), 1.0, 0.0)
        return grown.astype(BF)

    heads, per = EXP * HEAD, REST * PARTS
    rests = EXP * per
    slot_b = slot.astype(BF)
    grow, grow_rest = spread(heads, HEAD), spread(rests, per)
    hit = dot(grow, slot_b) == (iota((heads, TOK), 0) % HEAD).astype(F32)
    hit_rest = dot(grow_rest, slot_b) == (iota((rests, TOK), 0) % REST + HEAD).astype(F32)
    hi, lo = split2(gate)

    def weighted(grown, hits):
        pair = [jnp.where(hits, dot(grown, part), 0.0).T for part in (hi, lo)]
        return jnp.concatenate(pair, axis=0).astype(BF)

    pick_ref[...] = weighted(grow, hit)
    rest_ref[...] = weighted(grow_rest, hit_rest)
    dots = dots_ref[...].astype(F32)[:, BLOCK, :CAP]
    inner = jnp.zeros((EXP, TOK), F32)
    for r in range(CAP):
        inner = inner + jnp.where(slot == float(r), dots[:, r : r + 1], 0.0)
    mean = jnp.sum(gate * inner, axis=0, keepdims=True)
    d_probs = mask * ((inner - mean) / chosen_sum)
    d_logits = probs * (d_probs - jnp.sum(probs * d_probs, axis=0, keepdims=True))
    one, rem = split2(d_logits)[0], d_logits
    rem = rem - one.astype(F32)
    two, three = split2(rem)
    logit_ref[...] = jnp.concatenate([one, two, three], axis=0)


def gates(routing, base, small):
    heads, rests = EXP * HEAD, EXP * PER
    return pl.pallas_call(
        gate_kernel,
        out_shape=(
            jax.ShapeDtypeStruct((2 * TOK, heads), BF),
            jax.ShapeDtypeStruct((2 * TOK, rests), BF),
            jax.ShapeDtypeStruct((3 * EXP, TOK), BF),
        ),
        grid=(1,),
        in_specs=[
            full(4, TOK),
            full(EXP, TOK),
            full(EXP, BLOCK + ROOM, LANES),
        ],
        out_specs=(full(2 * TOK, heads), full(2 * TOK, rests), full(3 * EXP, TOK)),
        compiler_params=params(16),
        cost_estimate=cost(10**8, 10**6),
        name="gates",
    )(routing, base, small)


STEP = 4


def combine_kernel(
    pick_ref, rest_ref, logit_ref, cot_ref, head_ref, tail_ref, w_ref, router_ref, out_ref
):
    rests = EXP * PER
    piece = (iota((2 * TOK, rests), 1) % PER) // REST
    picked = rest_ref[...].astype(F32)
    tail = tail_ref[...].reshape(rests, COLS)
    router = jnp.concatenate([router_ref[...]] * 3, axis=0)
    total = dot(cot_ref[...], w_ref[...], 1, 1) + dot(logit_ref[...], router, 0, 0)
    for i in range(STEP):
        q = pl.program_id(0) * STEP + i
        rest = jnp.where(piece == q, picked, 0.0).astype(BF)
        head = head_ref[:, i * HEAD : (i + 1) * HEAD, :].reshape(EXP * HEAD, COLS)
        mixed = dot(pick_ref[...], head) + dot(rest, tail)
        at = slice(i * COLS, (i + 1) * COLS)
        out_ref[:, at] = (total[:, at] + mixed[:TOK] + mixed[TOK:]).astype(BF)


def combine(pick, rest, logit, cot, rows, w, router):
    heads, rests, wide = EXP * HEAD, EXP * PER, STEP * COLS
    return pl.pallas_call(
        combine_kernel,
        grid=(PARTS // STEP,),
        out_shape=jax.ShapeDtypeStruct((TOK, D), BF),
        in_specs=[
            full(2 * TOK, heads),
            full(2 * TOK, rests),
            full(3 * EXP, TOK),
            full(TOK, KC),
            pl.BlockSpec((EXP, STEP * HEAD, COLS), lambda q: (0, q, 0)),
            pl.BlockSpec((EXP, PER, COLS), lambda q: (0, PARTS * HEAD // PER, 0)),
            pl.BlockSpec((wide, KC), lambda q: (q, 0)),
            pl.BlockSpec((EXP, wide), lambda q: (0, q)),
        ],
        out_specs=pl.BlockSpec((TOK, wide), lambda q: (0, q)),
        compiler_params=params(BIG),
        cost_estimate=cost(2 * 10**9, 8 * 10**6),
        name="combine",
    )(pick, rest, logit, cot, rows, rows, w, router)


PIECES = [
    (tile, span)
    for tile in range(TILES)
    for span in range(SPAN)
    if tile * SUB < (span + 1) * LINE and (tile + 1) * SUB > span * LINE
]


def terms_kernel(core_ref, attn_ref, attn2_ref, cot_ref, cot2_ref, out_ref, moves):
    tall, wide = 2 * EXP * LINE, 2 * DPROWS

    @pl.when(pl.program_id(0) == 0)
    def _():
        to, fr = iota((tall, wide), 0), iota((tall, wide), 1)
        expert, pair, line = to // (2 * LINE), (to // LINE) % 2, to % LINE
        same = (fr // DPROWS == pair) & ((fr % DPROWS) // SUB == expert)
        for n, (tile, span) in enumerate(PIECES):
            hit = same & (tile * SUB + fr % SUB == span * LINE + line)
            moves[n] = jnp.where(hit, 1.0, 0.0).astype(BF)

    first = core_ref[0] == 0
    attn = jnp.concatenate([attn_ref[...], attn2_ref[...]], axis=0)
    cot = jnp.concatenate([cot_ref[...], cot2_ref[...]], axis=0)
    grad = dot(attn, cot, 0, 0)
    kept = []
    for j in range(8):
        zero = grad[2 * j * DPROWS : (2 * j + 1) * DPROWS]
        one = grad[(2 * j + 1) * DPROWS : (2 * j + 2) * DPROWS]
        kept.append(jnp.where(first, zero, one).astype(BF))
    pairs = [jnp.concatenate(kept[2 * i : 2 * i + 2], axis=0) for i in range(4)]
    spans = [jnp.zeros((tall, 4 * LANES), F32)] * SPAN
    for n, (tile, span) in enumerate(PIECES):
        at = slice(tile * LANES, (tile + 1) * LANES)
        both = jnp.concatenate([pair[:, at] for pair in pairs], axis=1)
        spans[span] = spans[span] + dot(moves[n], both)
    for i in range(4):
        at = slice(i * LANES, (i + 1) * LANES)
        out = jnp.concatenate([span[:, at] for span in spans], axis=1).astype(BF)
        out_ref[:, i * 2 * LINE : (i + 1) * 2 * LINE, :] = out.reshape(EXP, 2 * LINE, COLS)


def key_terms(core, attn, attn2, cot, cot2):
    columns = pl.BlockSpec((TOK, 8 * CORES * DPROWS), lambda i: (0, i))
    return pl.pallas_call(
        terms_kernel,
        grid=(ZN // 8,),
        out_shape=jax.ShapeDtypeStruct((EXP, KEYS, COLS), BF),
        in_specs=[smem(), columns, columns, full(TOK, KC), full(TOK, KC)],
        out_specs=pl.BlockSpec((EXP, 8 * LINE, COLS), lambda i: (0, i, 0)),
        scratch_shapes=[VM((len(PIECES), 2 * EXP * LINE, 2 * DPROWS), BF)],
        compiler_params=params(BIG),
        cost_estimate=cost(10**6, 2 * 10**6),
        name="key_terms",
    )(core, attn, attn2, cot, cot2)


def near_kernel(place_ref, terms_ref, *refs):
    *outs, total_ref = refs
    total = jnp.sum(terms_ref[...].astype(F32), axis=0)
    total_ref[...] = total.reshape(ZN, LINE, COLS)
    for rel in range(4):
        for a in range(FAR):
            outs[rel][a] = total_ref[4 * a + lax.rem(place_ref[0] + rel, 4)]


def near_terms(place, terms):
    return pl.pallas_call(
        near_kernel,
        in_specs=[smem(), vmem()],
        out_specs=[vmem()] * 4,
        out_shape=(jax.ShapeDtypeStruct((FAR, LINE, COLS), F32),) * 4,
        scratch_shapes=[VM((ZN, LINE, COLS), F32)],
        compiler_params=params(16),
        cost_estimate=cost(10**6, 2 * 10**6),
        name="near_terms",
    )(place, terms)


def far_kernel(place_ref, own_ref, up_ref, across_ref, down_ref, *outs):
    for rel in range(FAR):
        at = lax.rem(place_ref[0] + rel, FAR)
        outs[rel][...] = own_ref[at] + up_ref[at] + (across_ref[at] + down_ref[at])


def far_terms(place, *given):
    return pl.pallas_call(
        far_kernel,
        in_specs=[smem()] + [vmem()] * 4,
        out_specs=[vmem()] * 4,
        out_shape=(jax.ShapeDtypeStruct((LINE, COLS), F32),) * 4,
        compiler_params=params(16),
        cost_estimate=cost(10**6, 10**6),
        name="far_terms",
    )(place, *given)


def vmem():
    return pl.BlockSpec(memory_space=VM)


def adamw_kernel(own_ref, up_ref, across_ref, down_ref, weight_ref, first_ref, second_ref, *outs):
    total = own_ref[...] + up_ref[...] + (across_ref[...] + down_ref[...])
    total = [total[:, i * LANES : (i + 1) * LANES] for i in range(SPAN)]
    total = jnp.concatenate(total, axis=0)
    grad = jnp.concatenate([total[i * SUB : (i + 1) * SUB] for i in range(TILES)], axis=1)
    for out, value in zip(outs, adamw(weight_ref[...], first_ref[...], second_ref[...], grad)):
        out[...] = value


def update(*given):
    return pl.pallas_call(
        adamw_kernel,
        in_specs=[vmem()] * 7,
        out_specs=[vmem()] * 3,
        out_shape=(jax.ShapeDtypeStruct((SUB, KC), F32),) * 3,
        compiler_params=params(16),
        cost_estimate=cost(10**6, 10**6),
        name="adamw",
    )(*given)


def small_kernel(weight_ref, dots_ref, out_ref):
    weight = weight_ref[...]
    tall = jnp.concatenate([weight[:, i * LANES : (i + 1) * LANES] for i in range(TILES)], axis=0)
    to, fr = iota((EXP * ROOM, EXP), 0), iota((EXP * ROOM, EXP), 1)
    dots = jnp.concatenate([dots_ref[...], jnp.zeros((EXP, LANES - CAP), BF)], axis=1)
    spread = dot(jnp.where(to == fr * ROOM, 1.0, 0.0).astype(BF), dots)
    spread = spread.reshape(EXP, ROOM, LANES)
    tall = jnp.broadcast_to(tall[None], (EXP, BLOCK, LANES))
    out_ref[...] = jnp.concatenate([tall, spread], axis=1).astype(BF)


def small_block(weight, dots):
    return pl.pallas_call(
        small_kernel,
        in_specs=[vmem()] * 2,
        out_specs=vmem(),
        out_shape=jax.ShapeDtypeStruct((EXP, BLOCK + ROOM, LANES), BF),
        compiler_params=params(BIG),
        cost_estimate=cost(10**6, 10**6),
        name="small_block",
    )(weight, dots)


def order_kernel(small_ref, out_ref):
    size = EXP * (BLOCK + ROOM)
    blocks = small_ref[...].reshape(size, LANES)
    fr = iota((1, size), 1)
    expert, inside = fr // (BLOCK + ROOM), fr % (BLOCK + ROOM)
    row = expert * SUB + inside % SUB
    to = iota((DPROWS, size), 0)
    for i in range(TILES):
        move = jnp.where(jnp.where(inside // SUB == i, row, -1) == to, 1.0, 0.0).astype(BF)
        out_ref[:, i * LANES : (i + 1) * LANES] = dot(move, blocks).astype(BF)


def order_rows(small):
    return pl.pallas_call(
        order_kernel,
        in_specs=[vmem()],
        out_specs=vmem(),
        out_shape=jax.ShapeDtypeStruct((DPROWS, KC), BF),
        compiler_params=params(16),
        cost_estimate=cost(10**8, 10**6),
        name="order_key_rows",
    )(small)


def adamw(weight, first, second, grad):
    new_first = beta_one * first + (1.0 - beta_one) * grad
    new_second = beta_two * second + (1.0 - beta_two) * grad * grad
    first_hat = new_first / (1.0 - beta_one**ADAM_STEP)
    second_hat = new_second / (1.0 - beta_two**ADAM_STEP)
    new_weight = weight - learn_rate * (
        first_hat / (jnp.sqrt(second_hat) + epsilon) + decay_rate * weight
    )
    return (new_weight, new_first, new_second)


def exchange(x):
    return lax.all_to_all(x, "expert", split_axis=0, concat_axis=0, tiled=True)


def shift(x, step):
    pairs = [(i, ((i // CORES + step) % ZN) * CORES + i % CORES) for i in range(ZN * CORES)]
    return lax.ppermute(x, "dp", pairs)


def swap_core(x):
    return lax.ppermute(x, "dp", [(i, i ^ 1) for i in range(ZN * CORES)])


def local(
    attn_input,
    key_cot,
    routing,
    router_base,
    router_weight,
    expert_rows,
    expert_dots,
    key_weight,
    first_moment,
    second_moment,
):
    dp = lax.axis_index("dp")
    core, z = lax.rem(dp, CORES)[None], dp // CORES
    near_place, far_place = lax.rem(z, 4)[None], (z // 4)[None]
    small = exchange(small_block(key_weight, expert_dots))
    terms = key_terms(core, attn_input, swap_core(attn_input), key_cot, swap_core(key_cot))
    small, terms = lax.optimization_barrier((small, terms))
    w = lax.all_gather(order_rows(small), "dp", axis=0, tiled=True)
    terms, own_rows = lax.optimization_barrier((terms, expert_rows))
    terms = exchange(terms)
    packed = pack(jnp.swapaxes(own_rows, 0, 1))
    terms, packed = lax.optimization_barrier((terms, packed))
    rows = exchange(packed)
    own, up, across, down = near_terms(near_place, terms)
    own, up, across, down = far_terms(
        far_place, own, shift(up, 1), shift(across, -2), shift(down, -1)
    )
    grads = own, shift(up, 4), shift(across, 8), shift(down, -4)
    updated = update(*grads, key_weight, first_moment, second_moment)
    pick, rest, logit = gates(routing.T, router_base.T, small)
    rows, pick, updated = lax.optimization_barrier((rows, pick, updated))
    input_grad = combine(pick, rest, logit, key_cot, rows, w, router_weight.T)
    return (input_grad, *updated)


def solution(mesh):
    split = P(("dp", "expert"))
    in_specs = (split,) * 4 + (P(),) + (split,) * 5
    return jax.shard_map(
        local, mesh=mesh, in_specs=in_specs, out_specs=(split,) * 4, check_vma=False
    )
```

```python
import jax
import jax.numpy as jnp
from jax import lax
from jax.experimental import pallas as pl
from jax.experimental.pallas import tpu as pltpu
from jax.sharding import PartitionSpec as P

ADAM_STEP = 10

beta_one = 0.9
beta_two = 0.95
epsilon = 1e-08
learn_rate = 0.005
decay_rate = 0.1
routed_offset = 3.5

BF = jnp.bfloat16
F32 = jnp.float32

TOK, D, KC = 128, 3072, 512
EXP, CAP = 16, 34
HEAD = 32
REST = CAP - HEAD
PARTS = 8
COLS = D // PARTS
PER = REST * PARTS
ROWS = PARTS * HEAD + PER
ZN, CORES, SUB = 16, 2, 6
DPROWS = EXP * SUB

LANES = 128
TILES = KC // LANES
BLOCK = SUB * TILES
FAR = 4
SPAN = COLS // LANES
LINE = BLOCK // SPAN
KEYS = ZN * LINE
ROOM = 8

VM = pltpu.VMEM
HB = pl.ANY


def iota(shape, dim):
    return lax.broadcasted_iota(jnp.int32, shape, dim)


def dot(a, b, ca=1, cb=0):
    return lax.dot_general(a, b, (((ca,), (cb,)), ((), ())), preferred_element_type=F32)


def params(mib):
    return pltpu.CompilerParams(vmem_limit_bytes=mib * 1024 * 1024)


def cost(flops, moved):
    return pl.CostEstimate(flops=flops // 100, bytes_accessed=moved // 100, transcendentals=0)


BIG = 56


def smem():
    return pl.BlockSpec(memory_space=pltpu.SMEM)


def full(*shape):
    return pl.BlockSpec(shape, lambda *_: (0,) * len(shape))


def pack_kernel(rows_ref, out_ref, rows_in, head_out, rest_out, in_sem, out_sem):
    def fetch(q):
        return pltpu.make_async_copy(
            rows_ref.at[:, :, pl.ds(q * COLS, COLS)], rows_in.at[q], in_sem.at[q]
        )

    def put(q):
        return pltpu.make_async_copy(
            head_out.at[q], out_ref.at[:, pl.ds(q * HEAD, HEAD), :], out_sem.at[q]
        )

    for q in range(PARTS):
        fetch(q).start()
    heads, rests = EXP * HEAD, EXP * PER
    to, fr = iota((heads, heads), 0), iota((heads, heads), 1)
    move = jnp.where((to % HEAD) * EXP + to // HEAD == fr, 1.0, 0.0).astype(BF)
    to, fr = iota((rests, rests), 0), iota((rests, rests), 1)
    move_rest = jnp.where((to % PER) * EXP + to // PER == fr, 1.0, 0.0).astype(BF)
    rest = []
    for q in range(PARTS):
        fetch(q).wait()
        block = rows_in[q].reshape(CAP * EXP, COLS)
        head = dot(move, block[: HEAD * EXP])
        head_out[q] = head.astype(BF).reshape(EXP, HEAD, COLS)
        put(q).start()
        rest.append(block[HEAD * EXP :])
    rest = dot(move_rest, jnp.concatenate(rest, axis=0))
    rest_out[...] = rest.astype(BF).reshape(EXP, PER, COLS)
    last = pltpu.make_async_copy(
        rest_out, out_ref.at[:, pl.ds(PARTS * HEAD, PER), :], out_sem.at[PARTS]
    )
    last.start()
    for q in range(PARTS):
        put(q).wait()
    last.wait()


def pack(rows):
    return pl.pallas_call(
        pack_kernel,
        out_shape=jax.ShapeDtypeStruct((EXP, ROWS, COLS), BF),
        in_specs=[pl.BlockSpec(memory_space=HB)],
        out_specs=pl.BlockSpec(memory_space=HB),
        scratch_shapes=[
            VM((PARTS, CAP, EXP, COLS), BF),
            VM((PARTS, EXP, HEAD, COLS), BF),
            VM((EXP, PER, COLS), BF),
            pltpu.SemaphoreType.DMA((PARTS,)),
            pltpu.SemaphoreType.DMA((PARTS + 1,)),
        ],
        compiler_params=params(BIG),
        cost_estimate=cost(2 * 512 * 512 * D, 2 * EXP * CAP * D * 2),
        name="pack_rows",
    )(rows)


def split2(x):
    hi = x.astype(BF)
    return hi, (x - hi.astype(F32)).astype(BF)


def gate_kernel(routing_ref, base_ref, dots_ref, pick_ref, rest_ref, logit_ref):
    experts = iota((EXP, TOK), 0)
    mask = jnp.zeros((EXP, TOK), F32)
    for k in range(4):
        mask = mask + jnp.where(routing_ref[k : k + 1, :] == experts, 1.0, 0.0)
    logits = base_ref[...] + routed_offset * mask
    raised = jnp.exp(logits - jnp.max(logits, axis=0, keepdims=True))
    probs = raised / jnp.sum(raised, axis=0, keepdims=True)
    chosen = probs * mask
    chosen_sum = jnp.sum(chosen, axis=0, keepdims=True)
    gate = chosen / chosen_sum
    earlier = jnp.where(iota((TOK, TOK), 0) < iota((TOK, TOK), 1), 1.0, 0.0).astype(BF)
    before = dot(mask.astype(BF), earlier)
    slot = jnp.where(mask > 0, before, -1.0)

    def spread(rows, per):
        grown = jnp.where(iota((rows, EXP), 0) // per == iota((rows, EXP), 1), 1.0, 0.0)
        return grown.astype(BF)

    heads, per = EXP * HEAD, REST * PARTS
    rests = EXP * per
    slot_b = slot.astype(BF)
    grow, grow_rest = spread(heads, HEAD), spread(rests, per)
    hit = dot(grow, slot_b) == (iota((heads, TOK), 0) % HEAD).astype(F32)
    hit_rest = dot(grow_rest, slot_b) == (iota((rests, TOK), 0) % REST + HEAD).astype(F32)
    hi, lo = split2(gate)

    def weighted(grown, hits):
        pair = [jnp.where(hits, dot(grown, part), 0.0).T for part in (hi, lo)]
        return jnp.concatenate(pair, axis=0).astype(BF)

    pick_ref[...] = weighted(grow, hit)
    rest_ref[...] = weighted(grow_rest, hit_rest)
    dots = dots_ref[...].astype(F32)[:, BLOCK, :CAP]
    inner = jnp.zeros((EXP, TOK), F32)
    for r in range(CAP):
        inner = inner + jnp.where(slot == float(r), dots[:, r : r + 1], 0.0)
    mean = jnp.sum(gate * inner, axis=0, keepdims=True)
    d_probs = mask * ((inner - mean) / chosen_sum)
    d_logits = probs * (d_probs - jnp.sum(probs * d_probs, axis=0, keepdims=True))
    one, rem = split2(d_logits)[0], d_logits
    rem = rem - one.astype(F32)
    two, three = split2(rem)
    logit_ref[...] = jnp.concatenate([one, two, three], axis=0)


def gates(routing, base, small):
    heads, rests = EXP * HEAD, EXP * PER
    return pl.pallas_call(
        gate_kernel,
        out_shape=(
            jax.ShapeDtypeStruct((2 * TOK, heads), BF),
            jax.ShapeDtypeStruct((2 * TOK, rests), BF),
            jax.ShapeDtypeStruct((3 * EXP, TOK), BF),
        ),
        grid=(1,),
        in_specs=[
            full(4, TOK),
            full(EXP, TOK),
            full(EXP, BLOCK + ROOM, LANES),
        ],
        out_specs=(full(2 * TOK, heads), full(2 * TOK, rests), full(3 * EXP, TOK)),
        compiler_params=params(16),
        cost_estimate=cost(10**8, 10**6),
        name="gates",
    )(routing, base, small)


STEP = 4


def combine_kernel(
    pick_ref, rest_ref, logit_ref, cot_ref, head_ref, tail_ref, w_ref, router_ref, out_ref
):
    rests = EXP * PER
    piece = (iota((2 * TOK, rests), 1) % PER) // REST
    picked = rest_ref[...].astype(F32)
    tail = tail_ref[...].reshape(rests, COLS)
    router = jnp.concatenate([router_ref[...]] * 3, axis=0)
    total = dot(cot_ref[...], w_ref[...], 1, 1) + dot(logit_ref[...], router, 0, 0)
    for i in range(STEP):
        q = pl.program_id(0) * STEP + i
        rest = jnp.where(piece == q, picked, 0.0).astype(BF)
        head = head_ref[:, i * HEAD : (i + 1) * HEAD, :].reshape(EXP * HEAD, COLS)
        mixed = dot(pick_ref[...], head) + dot(rest, tail)
        at = slice(i * COLS, (i + 1) * COLS)
        out_ref[:, at] = (total[:, at] + mixed[:TOK] + mixed[TOK:]).astype(BF)


def combine(pick, rest, logit, cot, rows, w, router):
    heads, rests, wide = EXP * HEAD, EXP * PER, STEP * COLS
    return pl.pallas_call(
        combine_kernel,
        grid=(PARTS // STEP,),
        out_shape=jax.ShapeDtypeStruct((TOK, D), BF),
        in_specs=[
            full(2 * TOK, heads),
            full(2 * TOK, rests),
            full(3 * EXP, TOK),
            full(TOK, KC),
            pl.BlockSpec((EXP, STEP * HEAD, COLS), lambda q: (0, q, 0)),
            pl.BlockSpec((EXP, PER, COLS), lambda q: (0, PARTS * HEAD // PER, 0)),
            pl.BlockSpec((wide, KC), lambda q: (q, 0)),
            pl.BlockSpec((EXP, wide), lambda q: (0, q)),
        ],
        out_specs=pl.BlockSpec((TOK, wide), lambda q: (0, q)),
        compiler_params=params(BIG),
        cost_estimate=cost(2 * 10**9, 8 * 10**6),
        name="combine",
    )(pick, rest, logit, cot, rows, rows, w, router)


PIECES = [
    (tile, span)
    for tile in range(TILES)
    for span in range(SPAN)
    if tile * SUB < (span + 1) * LINE and (tile + 1) * SUB > span * LINE
]


def terms_kernel(core_ref, attn_ref, attn2_ref, cot_ref, cot2_ref, out_ref, moves):
    tall, wide = 2 * EXP * LINE, 2 * DPROWS

    @pl.when(pl.program_id(0) == 0)
    def _():
        to, fr = iota((tall, wide), 0), iota((tall, wide), 1)
        expert, pair, line = to // (2 * LINE), (to // LINE) % 2, to % LINE
        same = (fr // DPROWS == pair) & ((fr % DPROWS) // SUB == expert)
        for n, (tile, span) in enumerate(PIECES):
            hit = same & (tile * SUB + fr % SUB == span * LINE + line)
            moves[n] = jnp.where(hit, 1.0, 0.0).astype(BF)

    first = core_ref[0] == 0
    attn = jnp.concatenate([attn_ref[...], attn2_ref[...]], axis=0)
    cot = jnp.concatenate([cot_ref[...], cot2_ref[...]], axis=0)
    grad = dot(attn, cot, 0, 0)
    kept = []
    for j in range(8):
        zero = grad[2 * j * DPROWS : (2 * j + 1) * DPROWS]
        one = grad[(2 * j + 1) * DPROWS : (2 * j + 2) * DPROWS]
        kept.append(jnp.where(first, zero, one).astype(BF))
    pairs = [jnp.concatenate(kept[2 * i : 2 * i + 2], axis=0) for i in range(4)]
    spans = [jnp.zeros((tall, 4 * LANES), F32)] * SPAN
    for n, (tile, span) in enumerate(PIECES):
        at = slice(tile * LANES, (tile + 1) * LANES)
        both = jnp.concatenate([pair[:, at] for pair in pairs], axis=1)
        spans[span] = spans[span] + dot(moves[n], both)
    for i in range(4):
        at = slice(i * LANES, (i + 1) * LANES)
        out = jnp.concatenate([span[:, at] for span in spans], axis=1).astype(BF)
        out_ref[:, i * 2 * LINE : (i + 1) * 2 * LINE, :] = out.reshape(EXP, 2 * LINE, COLS)


def key_terms(core, attn, cot, other):
    cot2 = pl.BlockSpec((TOK, KC), lambda i: (0, D // KC))
    columns = pl.BlockSpec((TOK, 8 * CORES * DPROWS), lambda i: (0, i))
    return pl.pallas_call(
        terms_kernel,
        grid=(ZN // 8,),
        out_shape=jax.ShapeDtypeStruct((EXP, KEYS, COLS), BF),
        in_specs=[smem(), columns, columns, full(TOK, KC), cot2],
        out_specs=pl.BlockSpec((EXP, 8 * LINE, COLS), lambda i: (0, i, 0)),
        scratch_shapes=[VM((len(PIECES), 2 * EXP * LINE, 2 * DPROWS), BF)],
        compiler_params=params(BIG),
        cost_estimate=cost(10**6, 2 * 10**6),
        name="key_terms",
    )(core, attn, other, cot, other)


def near_kernel(place_ref, terms_ref, *refs):
    *outs, total_ref = refs
    total = jnp.sum(terms_ref[...].astype(F32), axis=0)
    total_ref[...] = total.reshape(ZN, LINE, COLS)
    for rel in range(4):
        for a in range(FAR):
            outs[rel][a] = total_ref[4 * a + lax.rem(place_ref[0] + rel, 4)]


def near_terms(place, terms):
    return pl.pallas_call(
        near_kernel,
        in_specs=[smem(), vmem()],
        out_specs=[vmem()] * 4,
        out_shape=(jax.ShapeDtypeStruct((FAR, LINE, COLS), F32),) * 4,
        scratch_shapes=[VM((ZN, LINE, COLS), F32)],
        compiler_params=params(16),
        cost_estimate=cost(10**6, 2 * 10**6),
        name="near_terms",
    )(place, terms)


def far_kernel(place_ref, own_ref, up_ref, across_ref, down_ref, *outs):
    for rel in range(FAR):
        at = lax.rem(place_ref[0] + rel, FAR)
        outs[rel][...] = own_ref[at] + up_ref[at] + (across_ref[at] + down_ref[at])


def far_terms(place, *given):
    return pl.pallas_call(
        far_kernel,
        in_specs=[smem()] + [vmem()] * 4,
        out_specs=[vmem()] * 4,
        out_shape=(jax.ShapeDtypeStruct((LINE, COLS), F32),) * 4,
        compiler_params=params(16),
        cost_estimate=cost(10**6, 10**6),
        name="far_terms",
    )(place, *given)


def vmem():
    return pl.BlockSpec(memory_space=VM)


def adamw_kernel(own_ref, up_ref, across_ref, down_ref, weight_ref, first_ref, second_ref, *outs):
    total = own_ref[...] + up_ref[...] + (across_ref[...] + down_ref[...])
    total = [total[:, i * LANES : (i + 1) * LANES] for i in range(SPAN)]
    total = jnp.concatenate(total, axis=0)
    grad = jnp.concatenate([total[i * SUB : (i + 1) * SUB] for i in range(TILES)], axis=1)
    for out, value in zip(outs, adamw(weight_ref[...], first_ref[...], second_ref[...], grad)):
        out[...] = value


def update(*given):
    return pl.pallas_call(
        adamw_kernel,
        in_specs=[vmem()] * 7,
        out_specs=[vmem()] * 3,
        out_shape=(jax.ShapeDtypeStruct((SUB, KC), F32),) * 3,
        compiler_params=params(16),
        cost_estimate=cost(10**6, 10**6),
        name="adamw",
    )(*given)


def small_kernel(weight_ref, dots_ref, attn_ref, cot_ref, out_ref, joined_ref, sem):
    copies = []
    for i in range(4):
        at = pl.ds(i * (TOK // 4), TOK // 4)
        copies.append(
            pltpu.make_async_copy(attn_ref.at[at], joined_ref.at[at, pl.ds(0, D)], sem.at[i])
        )
    copies.append(pltpu.make_async_copy(cot_ref, joined_ref.at[:, pl.ds(D, KC)], sem.at[4]))
    for copy in copies:
        copy.start()
    weight = weight_ref[...]
    tall = jnp.concatenate([weight[:, i * LANES : (i + 1) * LANES] for i in range(TILES)], axis=0)
    to, fr = iota((EXP * ROOM, EXP), 0), iota((EXP * ROOM, EXP), 1)
    dots = jnp.concatenate([dots_ref[...], jnp.zeros((EXP, LANES - CAP), BF)], axis=1)
    spread = dot(jnp.where(to == fr * ROOM, 1.0, 0.0).astype(BF), dots)
    spread = spread.reshape(EXP, ROOM, LANES)
    tall = jnp.broadcast_to(tall[None], (EXP, BLOCK, LANES))
    out_ref[...] = jnp.concatenate([tall, spread], axis=1).astype(BF)
    for copy in copies:
        copy.wait()


def small_block(weight, dots, attn, cot):
    return pl.pallas_call(
        small_kernel,
        in_specs=[vmem()] * 2 + [pl.BlockSpec(memory_space=HB)] * 2,
        out_specs=[vmem(), pl.BlockSpec(memory_space=HB)],
        out_shape=(
            jax.ShapeDtypeStruct((EXP, BLOCK + ROOM, LANES), BF),
            jax.ShapeDtypeStruct((TOK, D + KC), BF),
        ),
        scratch_shapes=[pltpu.SemaphoreType.DMA((5,))],
        compiler_params=params(BIG),
        cost_estimate=cost(10**6, 10**6),
        name="small_block",
    )(weight, dots, attn, cot)


def order_kernel(small_ref, out_ref):
    size = EXP * (BLOCK + ROOM)
    blocks = small_ref[...].reshape(size, LANES)
    fr = iota((1, size), 1)
    expert, inside = fr // (BLOCK + ROOM), fr % (BLOCK + ROOM)
    row = expert * SUB + inside % SUB
    to = iota((DPROWS, size), 0)
    for i in range(TILES):
        move = jnp.where(jnp.where(inside // SUB == i, row, -1) == to, 1.0, 0.0).astype(BF)
        out_ref[:, i * LANES : (i + 1) * LANES] = dot(move, blocks).astype(BF)


def order_rows(small):
    return pl.pallas_call(
        order_kernel,
        in_specs=[vmem()],
        out_specs=vmem(),
        out_shape=jax.ShapeDtypeStruct((DPROWS, KC), BF),
        compiler_params=params(16),
        cost_estimate=cost(10**8, 10**6),
        name="order_key_rows",
    )(small)


def adamw(weight, first, second, grad):
    new_first = beta_one * first + (1.0 - beta_one) * grad
    new_second = beta_two * second + (1.0 - beta_two) * grad * grad
    first_hat = new_first / (1.0 - beta_one**ADAM_STEP)
    second_hat = new_second / (1.0 - beta_two**ADAM_STEP)
    new_weight = weight - learn_rate * (
        first_hat / (jnp.sqrt(second_hat) + epsilon) + decay_rate * weight
    )
    return (new_weight, new_first, new_second)


def exchange(x):
    return lax.all_to_all(x, "expert", split_axis=0, concat_axis=0, tiled=True)


def shift(x, step):
    pairs = [(i, ((i // CORES + step) % ZN) * CORES + i % CORES) for i in range(ZN * CORES)]
    return lax.ppermute(x, "dp", pairs)


def swap_core(x):
    return lax.ppermute(x, "dp", [(i, i ^ 1) for i in range(ZN * CORES)])


def local(
    attn_input,
    key_cot,
    routing,
    router_base,
    router_weight,
    expert_rows,
    expert_dots,
    key_weight,
    first_moment,
    second_moment,
):
    dp = lax.axis_index("dp")
    core, z = lax.rem(dp, CORES)[None], dp // CORES
    near_place, far_place = lax.rem(z, 4)[None], (z // 4)[None]
    small, joined = small_block(key_weight, expert_dots, attn_input, key_cot)
    small = exchange(small)
    terms = key_terms(core, attn_input, key_cot, swap_core(joined))
    small, terms = lax.optimization_barrier((small, terms))
    w = lax.all_gather(order_rows(small), "dp", axis=0, tiled=True)
    terms, own_rows = lax.optimization_barrier((terms, expert_rows))
    terms = exchange(terms)
    packed = pack(jnp.swapaxes(own_rows, 0, 1))
    terms, packed = lax.optimization_barrier((terms, packed))
    rows = exchange(packed)
    own, up, across, down = near_terms(near_place, terms)
    own, up, across, down = far_terms(
        far_place, own, shift(up, 1), shift(across, -2), shift(down, -1)
    )
    grads = own, shift(up, 4), shift(across, 8), shift(down, -4)
    updated = update(*grads, key_weight, first_moment, second_moment)
    pick, rest, logit = gates(routing.T, router_base.T, small)
    rows, pick, updated = lax.optimization_barrier((rows, pick, updated))
    input_grad = combine(pick, rest, logit, key_cot, rows, w, router_weight.T)
    return (input_grad, *updated)


def solution(mesh):
    split = P(("dp", "expert"))
    in_specs = (split,) * 4 + (P(),) + (split,) * 5
    return jax.shard_map(
        local, mesh=mesh, in_specs=in_specs, out_specs=(split,) * 4, check_vma=False
    )
```
